256 devices in a mesh: seq: 8 (over y_lo, x), vocab: 32 (over z, y_hi, core).
Axes of the slice: x: 4, y: 4 (y_hi: 2, y_lo: 2; y = y_hi * 2 + y_lo), z: 8, core: 2. Of those that a mesh axis runs over, the one named last changes fastest.
Arguments:
- hidden: bfloat16 [8, 32, 2, 16, 2048], P('seq', 'vocab'), may hold values from -4 to 4
- head_weight: bfloat16 [32768, 2048], P('vocab'), may hold values from -4 to 4
- targets: int32 [8, 32, 2, 16], P('seq', 'vocab'), may hold values from 0 to 32767
- span_counts: int32 [8, 32, 2], P('seq', 'vocab'), may hold values from 0 to 16, as said below
- send_counts: int32 [8, 32, 8], P('seq', 'vocab'), may hold values from 0 to 4, as said below
Outputs:
- loss_rows: float32 [8, 32, 16], P('seq', 'vocab')
- hidden_grad: bfloat16 [8, 32, 2, 16, 2048], P('seq', 'vocab')
- code_grad: bfloat16 [32768, 2048], P('vocab', 'seq')
The draws below stay inside these ranges and needn't reach their ends.
Inputs may be any that keep to these rules, and one draw needn't show every extreme that they name: `span_counts`: the two span counts of an owner sum to 16. `send_counts`: every entry is 0 or 4; each row owner receives exactly 16 rows in all; an owner's counts sum to the sum of its two span counts.
All inputs are finite; a program needn't handle non-finite values.
Results may differ from the reference program's by a relative error of at most 0.019.
Values may be sent and summed in bfloat16 or wider, within the bound.
A program may use at most 64 MiB of HBM per device.

```python
import math
import jax
import jax.numpy as jnp
import numpy as np
from jax import lax

D = 2048
V = 32768
SEQ_LEN = 16
CAP = 4
ROWS_DEV = 16
V_DEV = 1024
N_SEQ = 8
N_VOCAB = 32


def head_table(key, spread):
    inner = jax.random.fold_in(key, 101)
    gauss = jax.random.normal(jax.random.fold_in(inner, 1), (V, D), jnp.float32)
    scales = jnp.exp(spread * jax.random.uniform(jax.random.fold_in(inner, 3), (V, 1), jnp.float32, -1.0, 1.0))
    return 12.0 / math.sqrt(D) * scales * gauss


def column_order(key):
    return jax.random.permutation(key, N_SEQ)


def count_table(key):
    inner = jax.random.fold_in(key, 202)
    base = CAP // 2
    row_keys = jax.random.split(jax.random.fold_in(inner, 1), N_VOCAB)
    col_keys = jax.random.split(jax.random.fold_in(inner, 2), N_VOCAB)
    row_order = jax.vmap(column_order)(row_keys)
    col_order = jax.vmap(column_order)(col_keys)
    parity = (row_order[:, :, None] + col_order[:, None, :]) % 2
    amount = base + base * (1 - 2 * parity)
    return amount.transpose(1, 0, 2).astype(jnp.int32)


def draw_head_weight(key, part):
    weight = head_table(key, 0.0)
    return jnp.clip(weight, -4.0, 4.0).astype(jnp.bfloat16)


def draw_hidden(key, part):
    key = jax.random.fold_in(key, 5)
    shape = (N_SEQ, N_VOCAB, 2, SEQ_LEN, D)
    states = 0.25 * jax.random.normal(key, shape, jnp.float32)
    return jnp.clip(states, -4.0, 4.0).astype(jnp.bfloat16)


def draw_send_counts(key, part):
    table = count_table(key)
    return table


def draw_span_counts(key, part):
    table = count_table(key)
    key = jax.random.fold_in(key, 7)
    totals = jnp.sum(table, axis=2).astype(jnp.int32)
    lowest = jnp.maximum(totals - SEQ_LEN, 0)
    highest = jnp.minimum(totals, SEQ_LEN)
    first_part = jax.random.randint(key, totals.shape, lowest, highest + 1)
    flat_first = first_part.reshape(N_SEQ * N_VOCAB)
    flat_first = flat_first.at[0].set(highest.reshape(N_SEQ * N_VOCAB)[0])
    flat_first = flat_first.at[1].set(lowest.reshape(N_SEQ * N_VOCAB)[1])
    first_part = flat_first.reshape(N_SEQ, N_VOCAB)
    return jnp.stack([first_part, totals - first_part], axis=-1).astype(jnp.int32)


def set_ends(result, key, least, top_value):
    longest = result.shape.index(max(result.shape))
    spots = []
    for shift in (0, 1):
        where = [jax.random.randint(jax.random.fold_in(key, axis), (), 0, length) for axis, length in enumerate(result.shape)]
        where[longest] = (where[longest] + shift) % result.shape[longest]
        spots.append(tuple(where))
    return result.at[spots[0]].set(least).at[spots[1]].set(top_value)


def rank_table(number_of, lean):
    loads = [(1 << 20) // math.isqrt(grade ** lean) + 1 for grade in range(1, number_of + 1)]
    scale = 1 + sum(loads) // (1 << 30)
    return np.cumsum(np.array([max(1, weight // scale) for weight in loads]))


def ranked(rng, extent, count, lean):
    grid = rank_table(count, lean)
    pick = jax.random.randint(jax.random.fold_in(rng, 1), extent, 0, int(grid[count - 1]))
    rank = jnp.searchsorted(jnp.asarray(grid, jnp.int32), pick, side="right")
    return jax.random.permutation(jax.random.fold_in(rng, 2), count)[rank].astype(jnp.int32)


def setup_inputs(seed: int = 0) -> dict:
    streams_of = jax.random.split(jax.random.key(seed), 6)
    hidden = draw_hidden(jax.random.fold_in(streams_of[5], 71), 0)
    head_weight = draw_head_weight(jax.random.fold_in(streams_of[5], 71), 0)
    targets = set_ends(ranked(streams_of[2], (N_SEQ, N_VOCAB, 2, SEQ_LEN), V, 2), jax.random.fold_in(streams_of[2], 3), 0, V - 1).astype(jnp.int32)
    span_counts = draw_span_counts(jax.random.fold_in(streams_of[5], 71), 0)
    send_counts = draw_send_counts(jax.random.fold_in(streams_of[5], 71), 0)
    return dict(hidden=hidden, head_weight=head_weight, targets=targets, span_counts=span_counts, send_counts=send_counts)


loss_scale = 4.0

def reference(hidden, head_weight, targets, span_counts, send_counts):
    position = jnp.arange(2 * SEQ_LEN, dtype=jnp.int32)
    first_span = span_counts[..., 0:1]
    second_span = span_counts[..., 1:2]
    in_first = position < SEQ_LEN
    speech = jnp.where(in_first, position >= SEQ_LEN - first_span, position - SEQ_LEN >= SEQ_LEN - second_span)
    marked = jnp.where(speech, targets.reshape(N_SEQ, N_VOCAB, 2 * SEQ_LEN), -1).astype(jnp.int32)
    group_rows = hidden.reshape(N_SEQ, N_VOCAB * 2 * SEQ_LEN, D)
    group_marks = marked.reshape(N_SEQ, N_VOCAB * 2 * SEQ_LEN)
    vocab_index = jnp.arange(V, dtype=jnp.int32)
    head_shards = head_weight.reshape(N_VOCAB, V_DEV, D)
    row_number = N_VOCAB * 2 * SEQ_LEN

    def shard_grad(total, pair):
        shard_grads, shard_weight = pair
        part = jnp.dot(shard_grads, shard_weight, preferred_element_type=jnp.float32).astype(jnp.bfloat16)
        part = lax.optimization_barrier(part)
        return (total + part.astype(jnp.float32), None)

    def group_head(carry, block):
        block_rows, block_marks = block
        logits = lax.dot_general(block_rows, head_weight, (((1,), (1,)), ((), ())), preferred_element_type=jnp.float32)
        row_top = lax.optimization_barrier(jnp.max(logits, axis=1))
        row_total = lax.optimization_barrier(jnp.sum(jnp.exp(logits - row_top[:, None]), axis=1))
        log_total = row_top + jnp.log(row_total)
        target_hit = block_marks[:, None] == vocab_index[None, :]
        target_logit = lax.optimization_barrier(jnp.sum(jnp.where(target_hit, logits, 0.0), axis=1))
        valid_entries = block_marks >= 0
        row_loss = jnp.where(valid_entries, log_total - target_logit, 0.0)
        logit_grads = jnp.where(valid_entries[:, None], loss_scale * (jnp.exp(logits - log_total[:, None]) - target_hit.astype(jnp.float32)), 0.0).astype(jnp.bfloat16)
        grads_by_shard = logit_grads.reshape(row_number, N_VOCAB, V_DEV).transpose(1, 0, 2)
        grad_sum, _ = lax.scan(shard_grad, jnp.zeros((row_number, D), jnp.float32), (grads_by_shard, head_shards))
        row_grad = grad_sum.astype(jnp.bfloat16)
        code_part = lax.dot_general(logit_grads, block_rows, (((0,), (0,)), ((), ())), preferred_element_type=jnp.float32).astype(jnp.bfloat16)
        code_part = lax.optimization_barrier(code_part)
        return (carry + code_part.astype(jnp.float32), (row_loss, row_grad))
    code_sum, (source_loss, source_grad) = lax.scan(group_head, jnp.zeros((V, D), jnp.float32), (group_rows, group_marks))
    source_loss = source_loss.reshape(N_SEQ, N_VOCAB, 2 * SEQ_LEN)
    rank_place = jnp.where(position < first_span, SEQ_LEN - first_span + position, 2 * SEQ_LEN - second_span + position - first_span)
    rank_place = jnp.clip(rank_place, 0, 2 * SEQ_LEN - 1).astype(jnp.int32)
    loss_by_rank = jnp.take_along_axis(source_loss, rank_place, axis=2)
    offsets = (jnp.cumsum(send_counts, axis=2) - send_counts).astype(jnp.int32)
    slot_index = jnp.arange(CAP, dtype=jnp.int32)
    slot_rank = jnp.clip(offsets[..., None] + slot_index, 0, 2 * SEQ_LEN - 1).astype(jnp.int32)
    slot_live = slot_index < send_counts[..., None]
    spread_loss = jnp.broadcast_to(loss_by_rank[:, :, None, :], (N_SEQ, N_VOCAB, N_SEQ, 2 * SEQ_LEN))
    slot_loss = jnp.where(slot_live, jnp.take_along_axis(spread_loss, slot_rank, axis=3), 0.0)
    slot_loss = slot_loss.transpose(2, 1, 0, 3).reshape(N_SEQ, N_VOCAB, N_SEQ * CAP)
    live_flags = slot_live.transpose(2, 1, 0, 3).reshape(N_SEQ, N_VOCAB, N_SEQ * CAP).astype(jnp.int32)
    before = (jnp.cumsum(live_flags, axis=2) - live_flags).astype(jnp.int32)
    row_index = jnp.arange(ROWS_DEV, dtype=jnp.int32)
    chosen = (live_flags[:, :, None, :] > 0) & (before[:, :, None, :] == row_index[None, None, :, None])
    loss_rows = lax.optimization_barrier(jnp.sum(jnp.where(chosen, slot_loss[:, :, None, :], 0.0), axis=3))
    return (loss_rows, source_grad.reshape(N_SEQ, N_VOCAB, 2, SEQ_LEN, D), code_sum.astype(jnp.bfloat16))
```

```python
import itertools

import jax
import jax.numpy as jnp
from jax import lax
from jax.experimental import pallas as pl
from jax.experimental.pallas import tpu as pltpu
from jax.sharding import PartitionSpec as P

LOSS_SCALE = 4.0
D = 2048
VD = 1024
RD = 16
NV = 32
R = RD * NV
NS = 8
CW = D // NS
HX = D + 128
Y_CHUNKS = [(112 * k, 112) for k in range(4)]
X_CHUNKS = [(448 + 144 * k, 144) for k in range(4)]
F32, BF16 = jnp.float32, jnp.bfloat16
MESH = pl.DeviceIdType.MESH


def nt(a, b):
    return lax.dot_general(a, b, (((1,), (1,)), ((), ())), preferred_element_type=F32)


def nn(a, b):
    return jnp.dot(a, b, preferred_element_type=F32)


def body(
    spans, counts, targets, hidden, weight,
    code_out, hid_out, loss_out,
    w, hx, lg, gt, g,
    st_mine, st_in, tot_mine, tot_in, loss_mine, loss_in,
    cp, y_in, xa_in, xl_in, xr_in, xx_a, xx_l, xx_r, yy_in, xs, xxs,
    hd_out, hd_in, hacc, za_out, za_in, zl_in, zr_in, zh_out, zh_in,
    ssem, rsem, wsem,
):
    me_s, me_v = lax.axis_index("seq"), lax.axis_index("vocab")
    x, y = lax.rem(me_s, 4), me_s // 4
    z, h, c = me_v // 4, lax.rem(me_v // 2, 2), lax.rem(me_v, 2)
    ids = itertools.count()
    sent = []

    def at(xx=None, yy=None, zz=None, hh=None, cc=None):
        xx, yy, zz, hh, cc = (
            mine if other is None else other
            for other, mine in ((xx, x), (yy, y), (zz, z), (hh, h), (cc, c))
        )
        return {"seq": yy * 4 + xx, "vocab": zz * 4 + hh * 2 + cc}

    def send(src, dst, device):
        i = next(ids)
        copy = pltpu.make_async_remote_copy(
            src_ref=src, dst_ref=dst, send_sem=ssem.at[i], recv_sem=rsem.at[i],
            device_id=device, device_id_type=MESH,
        )
        copy.start()
        sent.append(copy)
        return i, device

    def arrive(ticket, where):
        i, device = ticket
        pltpu.make_async_remote_copy(
            src_ref=where, dst_ref=where, send_sem=ssem.at[i], recv_sem=rsem.at[i],
            device_id=device, device_id_type=MESH,
        ).wait_recv()

    right_x, left_x, far_x = (lax.rem(x + k, 4) for k in (1, 3, 2))
    zs = [lax.rem(z + k, 8) for k in range(8)]
    other_c, other_h, other_y = at(cc=1 - c), at(hh=1 - h), at(yy=1 - y)
    layer = [other_c, other_h, at(hh=1 - h, cc=1 - c)]
    column = [at(zz=zs[k]) for k in range(1, 8)]
    others = [
        {"seq": lax.rem(me_s + k, NS), "vocab": me_v} for k in range(1, NS)
    ]

    weight_in = pltpu.make_async_copy(weight, w, wsem)
    weight_in.start()
    barrier = pltpu.get_barrier_semaphore()
    for device in layer + column + others:
        pl.semaphore_signal(barrier, inc=1, device_id=device, device_id_type=MESH)

    s0 = spans[0, 0, 0]

    def position(shape):
        rank = lax.broadcasted_iota(jnp.int32, shape, 0)
        return jnp.where(rank < s0, RD - s0 + rank, RD + rank)

    pick = (position((RD, 2 * RD)) == lax.broadcasted_iota(jnp.int32, (RD, 2 * RD), 1)).astype(F32).astype(BF16)
    packed = nn(pick, hidden[0, 0].reshape(2 * RD, D)).astype(BF16)
    place = position((RD, 128))
    code = jnp.zeros((RD, 128), jnp.int32)
    for q in range(2):
        for p in range(RD):
            code = jnp.where(place == q * RD + p, targets[0, 0, q, p], code)
    lane = lax.broadcasted_iota(jnp.int32, (RD, 128), 1)
    extra = jnp.where(lane == 0, code // 256, jnp.where(lane == 1, lax.rem(code, 256), 0))

    def rows(zz, hh, cc):
        return pl.ds(pl.multiple_of(cc * 256 + zz * 32 + hh * 16, 16), 16)

    def block(zz, hh, cc=c):
        return hx.at[rows(zz, hh, cc)]

    mine = block(z, h)
    hx[rows(z, h, c), 0:D] = packed
    hx[rows(z, h, c), D:HX] = extra.astype(F32).astype(BF16)
    pl.semaphore_wait(barrier, len(layer + column + others))

    up, down = at(zz=zs[1]), at(zz=zs[7])
    hs = (h, 1 - h)
    from_y = send(mine, mine, other_h)
    ups, downs = [None, None], [None, None]
    crossed = []

    def cross(zz, hh):
        crossed.append((send(block(zz, hh), block(zz, hh), other_c), zz, hh))

    ups[0], downs[0] = send(mine, mine, up), send(mine, mine, down)
    cross(z, h)
    arrive(from_y, block(z, 1 - h))
    other = block(z, 1 - h)
    ups[1], downs[1] = send(other, other, up), send(other, other, down)
    cross(z, 1 - h)
    for k in range(1, 5):
        below, above = zs[8 - k], zs[k]
        next_ups, next_downs = [None, None], [None, None]
        for b in range(2):
            if ups[b] is not None:
                here = block(below, hs[b])
                arrive(ups[b], here)
                if k < 3 or (k == 3 and b == 0):
                    next_ups[b] = send(here, here, up)
                cross(below, hs[b])
            if downs[b] is not None:
                here = block(above, hs[b])
                arrive(downs[b], here)
                if k < 3 or (k == 3 and b == 1):
                    next_downs[b] = send(here, here, down)
                cross(above, hs[b])
        ups, downs = next_ups, next_downs
    for ticket, zz, hh in crossed:
        arrive(ticket, block(zz, hh, 1 - c))
    weight_in.wait()

    def logits_of(k, _):
        at_k = pl.ds(pl.multiple_of(k * 256, 256), 256)
        lg[at_k, :] = nt(w[at_k, :], hx[:, 0:D])
        return 0

    lax.fori_loop(0, VD // 256, logits_of, 0)

    ones = lax.broadcasted_iota(jnp.int32, (8, 128), 0) == lax.broadcasted_iota(jnp.int32, (8, 128), 1)
    halves = nt(ones.astype(F32).astype(BF16), hx[:, D:HX])
    marked = (halves[0:1] * 256.0 + halves[1:2]).astype(jnp.int32) - me_v * VD
    top = jnp.max(lg[...], axis=0, keepdims=True)

    def sums_of(k, carry):
        total, named = carry
        at_k = pl.ds(pl.multiple_of(k * 64, 64), 64)
        part = lg[at_k, :]
        code_at = lax.broadcasted_iota(jnp.int32, (64, R), 0) + k * 64
        named = named + jnp.sum(jnp.where(code_at == marked, part, 0.0), axis=0, keepdims=True)
        grown = jnp.exp(part - top)
        lg[at_k, :] = grown
        return total + jnp.sum(grown, axis=0, keepdims=True), named

    total, named = lax.fori_loop(
        0, VD // 64, sums_of, (jnp.zeros((1, R), F32), jnp.zeros((1, R), F32))
    )

    def fold(row):
        return [row[:, 128 * k : 128 * (k + 1)] for k in range(R // 128)]

    def join(tops, totals, nameds):
        best = tops[0]
        for other_top in tops[1:]:
            best = jnp.maximum(best, other_top)
        total = sum(t * jnp.exp(m - best) for t, m in zip(totals, tops))
        return best, total, sum(nameds)

    def exchange(triple, out_ref, in_ref, devices):
        out_ref[0:4], out_ref[4:8], out_ref[8:12] = triple
        out_ref[12:16] = jnp.zeros((4, 128), F32)
        tickets = [send(out_ref, in_ref.at[k], device) for k, device in enumerate(devices)]
        for k, ticket in enumerate(tickets):
            arrive(ticket, in_ref.at[k])
        parts = [triple] + [
            (in_ref[k, 0:4], in_ref[k, 4:8], in_ref[k, 8:12]) for k in range(len(devices))
        ]
        return join(*zip(*parts))

    triple = tuple(jnp.concatenate(fold(row), axis=0) for row in (top, total, named))
    triple = exchange(triple, st_mine, st_in, layer)
    row_top, row_total, row_named = exchange(triple, tot_mine, tot_in, column)
    log_total = row_top + jnp.log(row_total)
    loss_mine[0:4] = log_total - row_named
    lanes8 = lax.broadcasted_iota(jnp.int32, (4, 128), 1)
    sends = jnp.zeros((4, 128), F32)
    for j in range(NS):
        sends = jnp.where(lanes8 == j, counts[0, 0, j].astype(F32), sends)
    loss_mine[4:8] = sends
    loss_tickets = [send(loss_mine, loss_in.at[k], device) for k, device in enumerate(others)]

    factor = LOSS_SCALE * jnp.exp(
        top - jnp.concatenate([log_total[k : k + 1] for k in range(R // 128)], axis=1)
    )

    def grads_of(start, size):
        code_at = lax.broadcasted_iota(jnp.int32, (size, R), 0) + start
        grad = lg[start : start + size, :] * factor - jnp.where(code_at == marked, LOSS_SCALE, 0.0)
        gt[start : start + size, :] = grad.astype(BF16)

    def part(chunk, s):
        start, size = chunk
        return nn(gt[start : start + size, :], hx[:, pl.ds(pl.multiple_of(s * CW, CW), CW)])

    y_tickets = []
    for k, chunk in enumerate(Y_CHUNKS):
        start, size = chunk
        grads_of(start, size)
        for xx in range(4):
            cp[xx, start : start + size, :] = part(chunk, (1 - y) * 4 + xx).astype(BF16)
        y_tickets.append(send(cp.at[:, start : start + size], y_in.at[:, start : start + size], other_y))
    first_x = X_CHUNKS[0][0]
    a_tickets = []
    for k, chunk in enumerate(X_CHUNKS):
        start, size = chunk
        grads_of(start, size)
        spot = slice(start - first_x, start - first_x + size)
        pair = []
        for q, device in enumerate((at(xx=right_x), at(xx=left_x))):
            xxs[q, spot, :] = part(chunk, q * 4 + far_x).astype(BF16)
            pair.append(send(xxs.at[q, spot], xx_a.at[q, spot], device))
        a_tickets.append(pair)

    def turn(k, _):
        at_k = pl.ds(pl.multiple_of(k * 256, 256), 256)
        g[:, at_k] = gt[at_k, :].astype(F32).T.astype(BF16)
        return 0

    lax.fori_loop(0, VD // 256, turn, 0)

    def core_rows(cc):
        return pl.ds(pl.multiple_of(cc * 256, 256), 256)

    def theirs(k, _):
        at_k = pl.ds(pl.multiple_of(k * 512, 512), 512)
        hd_out[:, at_k] = nn(g[core_rows(1 - c), :], w[:, at_k]).astype(BF16)
        return 0

    lax.fori_loop(0, D // 512, theirs, 0)
    d_ticket = send(hd_out, hd_in, other_c)

    lr_tickets = []
    for k, chunk in enumerate(X_CHUNKS):
        start, size = chunk
        spot = slice(start - first_x, start - first_x + size)
        pair = []
        for side, (to, into) in enumerate(((right_x, xx_l), (left_x, xx_r))):
            arrive(a_tickets[k][side], xx_a.at[side, spot])
            for q in range(2):
                value = part(chunk, q * 4 + to)
                if q == side:
                    value = value + xx_a[q, spot, :].astype(F32)
                xxs[2 + 2 * side + q, spot, :] = value.astype(BF16)
            pair.append(
                send(xxs.at[2 + 2 * side : 4 + 2 * side, spot], into.at[:, spot], at(xx=to))
            )
        lr_tickets.append(pair)

    arrive(d_ticket, hd_in)

    def ours(k, _):
        at_k = pl.ds(pl.multiple_of(k * 512, 512), 512)
        hacc[:, at_k] = nn(g[core_rows(c), :], w[:, at_k]) + hd_in[:, at_k].astype(F32)
        return 0

    lax.fori_loop(0, D // 512, ours, 0)

    def layer_rows(zz, first=0, size=32):
        return pl.ds(pl.multiple_of(zz * 32 + first, 16), size)

    za_out[0] = hacc[layer_rows(zs[4], 0, 16), :].astype(BF16)
    za_out[1] = hacc[layer_rows(zs[4], 16, 16), :].astype(BF16)
    z_up = send(za_out.at[0], za_in.at[0], up)
    z_down = send(za_out.at[1], za_in.at[1], down)

    def z_step(k, z_up, z_down):
        outs = []
        for side, (ticket, into, to, owner) in enumerate(
            ((z_up, zl_in, up, zs[4 - k]), (z_down, zr_in, down, zs[4 + k]))
        ):
            own = hacc[layer_rows(owner), :]
            if k == 1:
                arrive(ticket, za_in.at[side])
                other = za_in[side].astype(F32)
                if side == 0:
                    value = jnp.concatenate([own[0:16] + other, own[16:32]], axis=0)
                else:
                    value = jnp.concatenate([own[0:16], own[16:32] + other], axis=0)
            else:
                arrive(ticket, into.at[k - 2])
                value = own + into[k - 2].astype(F32)
            zh_out[side, k - 1] = value.astype(BF16)
            outs.append(send(zh_out.at[side, k - 1], into.at[k - 1], to))
        return outs

    yy_tickets = []
    for k, chunk in enumerate(X_CHUNKS):
        start, size = chunk
        spot = slice(start - first_x, start - first_x + size)
        arrive(lr_tickets[k][0], xx_l.at[:, spot])
        arrive(lr_tickets[k][1], xx_r.at[:, spot])
        value = part(chunk, (1 - y) * 4 + x)
        value = value + xx_l[1 - y, spot, :].astype(F32) + xx_r[1 - y, spot, :].astype(F32)
        xxs[6, spot, :] = value.astype(BF16)
        yy_tickets.append(send(xxs.at[6, spot], yy_in.at[spot], other_y))
        if k == 1:
            z_up, z_down = z_step(1, z_up, z_down)

    def y_arrived(chunk, xx):
        start, size = chunk
        return part(chunk, y * 4 + xx) + y_in[xx, start : start + size, :].astype(F32)

    xa_tickets, xlr_tickets = {}, {}

    def first_hop(k):
        start, size = Y_CHUNKS[k]
        half = size // 32 * 16
        arrive(y_tickets[k], y_in.at[:, start : start + size])
        xs[0, start : start + size, :] = y_arrived(Y_CHUNKS[k], far_x).astype(BF16)
        pair = []
        for spot, device in (
            (slice(start, start + half), at(xx=right_x)),
            (slice(start + half, start + size), at(xx=left_x)),
        ):
            pair.append((send(xs.at[0, spot], xa_in.at[spot], device), spot))
        xa_tickets[k] = pair

    def second_hop(k):
        start, size = Y_CHUNKS[k]
        half = size // 32 * 16
        all_rows = slice(start, start + size)
        pair = []
        for side, (to, into) in enumerate(((right_x, xl_in), (left_x, xr_in))):
            ticket, spot = xa_tickets[k][side]
            arrive(ticket, xa_in.at[spot])
            value = y_arrived(Y_CHUNKS[k], to)
            other = xa_in[spot, :].astype(F32)
            if side == 0:
                value = jnp.concatenate([value[:half] + other, value[half:]], axis=0)
            else:
                value = jnp.concatenate([value[:half], value[half:] + other], axis=0)
            xs[1 + side, all_rows, :] = value.astype(BF16)
            pair.append(send(xs.at[1 + side, all_rows], into.at[all_rows], at(xx=to)))
        xlr_tickets[k] = pair

    def y_finish(k):
        start, size = Y_CHUNKS[k]
        spot = slice(start, start + size)
        arrive(xlr_tickets[k][0], xl_in.at[spot])
        arrive(xlr_tickets[k][1], xr_in.at[spot])
        value = y_arrived(Y_CHUNKS[k], x)
        value = value + xl_in[spot, :].astype(F32) + xr_in[spot, :].astype(F32)
        code_out[spot, :] = value.astype(BF16)

    n = len(Y_CHUNKS)
    for k in range(n + 2):
        if k < n:
            first_hop(k)
        if k < 2:
            z_up, z_down = z_step(k + 2, z_up, z_down)
        if 0 <= k - 1 < n:
            second_hop(k - 1)
        if k == 2:
            arrive(z_up, zl_in.at[2])
            arrive(z_down, zr_in.at[2])
            summed = hacc[layer_rows(z), :] + zl_in[2].astype(F32) + zr_in[2].astype(F32)
            zh_in[1:3] = summed.reshape(2, RD, D)
            zh_out[0, 3, 0:16] = zh_in[1 + (1 - h)].astype(BF16)
            h_ticket = send(zh_out.at[0, 3, 0:16], za_in.at[2], other_h)
        if 0 <= k - 2 < n:
            y_finish(k - 2)

    for k, chunk in enumerate(X_CHUNKS):
        start, size = chunk
        spot = slice(start - first_x, start - first_x + size)
        arrive(yy_tickets[k], yy_in.at[spot])
        value = part(chunk, y * 4 + x) + yy_in[spot, :].astype(F32)
        value = value + xx_l[y, spot, :].astype(F32) + xx_r[y, spot, :].astype(F32)
        code_out[start : start + size, :] = value.astype(BF16)

    arrive(h_ticket, za_in.at[2])
    own = (zh_in[1 + h] + za_in[2].astype(F32)).astype(BF16)
    spread = (
        position_row(s0) == lax.broadcasted_iota(jnp.int32, (2 * RD, RD), 0)
    ).astype(F32).astype(BF16)
    hid_out[...] = nn(spread, own).astype(BF16)

    tiles = [loss_mine[...]]
    for k, ticket in enumerate(loss_tickets):
        arrive(ticket, loss_in.at[k])
        tiles.append(loss_in[k])
    lane1 = lax.broadcasted_iota(jnp.int32, (1, 128), 1)
    own_row = lax.broadcasted_iota(jnp.int32, (4, 128), 0) == (c * 2 + z // 4)
    rank = lane1 - (lax.rem(z, 4) * 32 + h * 16)
    in_block = (rank >= 0) & (rank < RD)
    slots = lax.broadcasted_iota(jnp.int32, (RD, 128), 0)
    got, before, losses = [], [], []
    for tile in tiles:
        row = tile[4:5]
        got.append(jnp.sum(jnp.where(lane1 == me_s, row, 0.0), axis=1, keepdims=True).astype(jnp.int32))
        before.append(jnp.sum(jnp.where(lane1 < me_s, row, 0.0), axis=1, keepdims=True).astype(jnp.int32))
        losses.append(jnp.sum(jnp.where(own_row, tile[0:4], 0.0), axis=0, keepdims=True))
    listed = jnp.zeros((RD, 128), F32)
    for k in range(NS):
        source = lax.rem(me_s + NS - k, NS)
        first = jnp.zeros((1, 1), jnp.int32)
        for j in range(NS):
            earlier = lax.rem(me_s + NS - j, NS) < source
            first = first + jnp.where(earlier, got[j], 0)
        offset = rank - before[k]
        live = in_block & (offset >= 0) & (offset < got[k])
        slot = jnp.where(live, first + offset, -1)
        listed = listed + jnp.where(slots == slot, losses[k], 0.0)
    loss_out[...] = listed

    for copy in sent:
        copy.wait_send()


def position_row(s0):
    rank = lax.broadcasted_iota(jnp.int32, (2 * RD, RD), 1)
    return jnp.where(rank < s0, RD - s0 + rank, RD + rank)


def per_device(hidden, head_weight, targets, span_counts, send_counts):
    ny = Y_CHUNKS[-1][0] + Y_CHUNKS[-1][1]
    nx = VD - ny
    vmem, smem = pl.BlockSpec(memory_space=pltpu.VMEM), pl.BlockSpec(memory_space=pltpu.SMEM)
    copies = 256
    code_grad, hidden_grad, listed = pl.pallas_call(
        body,
        out_shape=(
            jax.ShapeDtypeStruct((VD, CW), BF16),
            jax.ShapeDtypeStruct((2 * RD, D), BF16),
            jax.ShapeDtypeStruct((RD, 128), F32),
        ),
        in_specs=[smem, smem, smem, vmem, pl.BlockSpec(memory_space=pl.ANY)],
        out_specs=(vmem, vmem, vmem),
        scratch_shapes=[
            pltpu.VMEM((VD, D), BF16),
            pltpu.VMEM((R, HX), BF16),
            pltpu.VMEM((VD, R), F32),
            pltpu.VMEM((VD, R), BF16),
            pltpu.VMEM((R, VD), BF16),
            pltpu.VMEM((16, 128), F32),
            pltpu.VMEM((3, 16, 128), F32),
            pltpu.VMEM((16, 128), F32),
            pltpu.VMEM((7, 16, 128), F32),
            pltpu.VMEM((8, 128), F32),
            pltpu.VMEM((7, 8, 128), F32),
            pltpu.VMEM((4, ny, CW), BF16),
            pltpu.VMEM((4, ny, CW), BF16),
            pltpu.VMEM((ny, CW), BF16),
            pltpu.VMEM((ny, CW), BF16),
            pltpu.VMEM((ny, CW), BF16),
            pltpu.VMEM((2, nx, CW), BF16),
            pltpu.VMEM((2, nx, CW), BF16),
            pltpu.VMEM((2, nx, CW), BF16),
            pltpu.VMEM((nx, CW), BF16),
            pltpu.VMEM((3, ny, CW), BF16),
            pltpu.VMEM((7, nx, CW), BF16),
            pltpu.VMEM((256, D), BF16),
            pltpu.VMEM((256, D), BF16),
            pltpu.VMEM((256, D), F32),
            pltpu.VMEM((2, 16, D), BF16),
            pltpu.VMEM((3, 16, D), BF16),
            pltpu.VMEM((3, 32, D), BF16),
            pltpu.VMEM((3, 32, D), BF16),
            pltpu.VMEM((2, 4, 32, D), BF16),
            pltpu.VMEM((3, 16, D), F32),
            pltpu.SemaphoreType.DMA((copies,)),
            pltpu.SemaphoreType.DMA((copies,)),
            pltpu.SemaphoreType.DMA,
        ],
        compiler_params=pltpu.CompilerParams(
            collective_id=0, has_side_effects=True, vmem_limit_bytes=56 * 1024 * 1024
        ),
        name="head",
    )(span_counts, send_counts, targets, hidden, head_weight)
    return (
        jnp.sum(listed, axis=1).reshape(1, 1, RD),
        hidden_grad.reshape(hidden.shape),
        code_grad,
    )


def solution(mesh):
    in_specs = (
        P("seq", "vocab", None, None, None),
        P("vocab", None),
        P("seq", "vocab", None, None),
        P("seq", "vocab", None),
        P("seq", "vocab", None),
    )
    out_specs = (P("seq", "vocab", None), P("seq", "vocab", None, None, None), P("vocab", "seq"))
    return jax.shard_map(
        per_device, mesh=mesh, in_specs=in_specs, out_specs=out_specs, check_vma=False
    )
```

```python
import itertools

import jax
import jax.numpy as jnp
from jax import lax
from jax.experimental import pallas as pl
from jax.experimental.pallas import tpu as pltpu
from jax.sharding import PartitionSpec as P

LOSS_SCALE = 4.0
D = 2048
VD = 1024
RD = 16
NV = 32
R = RD * NV
NS = 8
CW = D // NS
HX = D + 128
CHUNKS = [(256 * k, 256) for k in range(4)]
FAR = (4, 3, 5, 2, 6, 1, 7, 0)
GROUPS = ((0, 1), (1, 3), (3, 5), (5, 8))
F32, BF16 = jnp.float32, jnp.bfloat16
MESH = pl.DeviceIdType.MESH


def nt(a, b):
    return lax.dot_general(a, b, (((1,), (1,)), ((), ())), preferred_element_type=F32)


def nn(a, b):
    return jnp.dot(a, b, preferred_element_type=F32)


def body(
    spans, counts, targets, hidden, weight,
    code_out, hid_out, loss_out,
    w, hx, lg, gt, g,
    st_mine, st_in, tot_mine, tot_in, lt_mine, lt_in, loss_mine, loss_in,
    xs, xa_in, xl_in, xr_in,
    hd_out, hd_in, hacc, yo, yi, zo, zi,
    ssem, rsem, wsem,
):
    me_s, me_v = lax.axis_index("seq"), lax.axis_index("vocab")
    x, y = lax.rem(me_s, 4), me_s // 4
    z, h, c = me_v // 4, lax.rem(me_v // 2, 2), lax.rem(me_v, 2)
    ids = itertools.count()
    sent = []

    def at(xx=None, yy=None, zz=None, hh=None, cc=None):
        xx, yy, zz, hh, cc = (
            mine if other is None else other
            for other, mine in ((xx, x), (yy, y), (zz, z), (hh, h), (cc, c))
        )
        return {"seq": yy * 4 + xx, "vocab": zz * 4 + hh * 2 + cc}

    def send(src, dst, device):
        i = next(ids)
        copy = pltpu.make_async_remote_copy(
            src_ref=src, dst_ref=dst, send_sem=ssem.at[i], recv_sem=rsem.at[i],
            device_id=device, device_id_type=MESH,
        )
        copy.start()
        sent.append(copy)
        return i, device

    def arrive(ticket, where):
        i, device = ticket
        pltpu.make_async_remote_copy(
            src_ref=where, dst_ref=where, send_sem=ssem.at[i], recv_sem=rsem.at[i],
            device_id=device, device_id_type=MESH,
        ).wait_recv()

    right_x, left_x, far_x = (lax.rem(x + k, 4) for k in (1, 3, 2))
    zs = [lax.rem(z + k, 8) for k in range(8)]
    other_c, other_h = at(cc=1 - c), at(hh=1 - h)
    near_y = [at(yy=1 - y), at(yy=1 - y, hh=1 - h)]
    layer = [other_c, other_h, at(hh=1 - h, cc=1 - c)]
    column = [at(zz=zs[k]) for k in range(1, 8)]
    others = [
        {"seq": lax.rem(me_s + k, NS), "vocab": me_v} for k in range(1, NS)
    ]
    peers = layer + column + others + near_y[1:]

    weight_in = pltpu.make_async_copy(weight, w, wsem)
    weight_in.start()
    barrier = pltpu.get_barrier_semaphore()
    for device in peers:
        pl.semaphore_signal(barrier, inc=1, device_id=device, device_id_type=MESH)

    s0 = spans[0, 0, 0]

    def position(shape, axis):
        rank = lax.broadcasted_iota(jnp.int32, shape, axis)
        return jnp.where(rank < s0, RD - s0 + rank, RD + rank)

    pick = position((RD, 2 * RD), 0) == lax.broadcasted_iota(jnp.int32, (RD, 2 * RD), 1)
    packed = nn(pick.astype(F32).astype(BF16), hidden[0, 0].reshape(2 * RD, D)).astype(BF16)
    place = position((RD, 128), 0)
    code = jnp.zeros((RD, 128), jnp.int32)
    for q in range(2):
        for p in range(RD):
            code = jnp.where(place == q * RD + p, targets[0, 0, q, p], code)
    lane = lax.broadcasted_iota(jnp.int32, (RD, 128), 1)
    extra = jnp.where(lane == 0, code // 256, jnp.where(lane == 1, lax.rem(code, 256), 0))

    def rows(zz, hh, cc, yy, size=16):
        return pl.ds(pl.multiple_of(yy * R + cc * 256 + zz * 32 + hh * 16, 16), size)

    def block(zz, hh, yy=y):
        return hx.at[rows(zz, hh, c, yy)]

    def pair(zz, cc=c, yy=y):
        return hx.at[rows(zz, 0, cc, yy, 32)]

    mine = block(z, h)
    hx[rows(z, h, c, y), 0:D] = packed
    hx[rows(z, h, c, y), D:HX] = extra.astype(F32).astype(BF16)
    pl.semaphore_wait(barrier, len(peers))

    up, down = at(zz=zs[1]), at(zz=zs[7])
    by_z, by_y, by_h = {}, {}, {}
    crossed = {}

    def cross(k, yy=y):
        crossed[k] = send(pair(zs[k], c, yy), pair(zs[k], c, yy), other_c)

    def spread_y(k):
        here = block(zs[k], h)
        by_y[k] = [send(here, here, device) for device in near_y]

    by_h[0] = send(mine, mine, other_h)
    for k in (4, 3, 5, 1, 7, 2, 6):
        by_z[(8 - k) % 8] = send(mine, mine, at(zz=zs[k]))
    spread_y(0)
    arrive(by_h[0], block(z, 1 - h))
    other = block(z, 1 - h)
    ups, downs = send(other, other, up), send(other, other, down)
    cross(0)
    for k in (4, 3, 5):
        here = block(zs[k], h)
        arrive(by_z[k], here)
        by_h[k] = send(here, here, other_h)
        spread_y(k)
    for k in (1, 7):
        arrive(by_z[k], block(zs[k], h))
        spread_y(k)
    here = block(zs[7], 1 - h)
    arrive(ups, here)
    ups = send(here, here, up)
    cross(7)
    here = block(zs[1], 1 - h)
    arrive(downs, here)
    downs = send(here, here, down)
    cross(1)
    for k in (2, 6):
        arrive(by_z[k], block(zs[k], h))
        spread_y(k)
    for k in (4, 3, 5):
        arrive(by_h[k], block(zs[k], 1 - h))
        cross(k)
    arrive(ups, block(zs[6], 1 - h))
    cross(6)
    arrive(downs, block(zs[2], 1 - h))
    cross(2)
    for k in (0, 7, 1, 4, 3, 5, 6, 2):
        arrive(crossed[k], pair(zs[k], 1 - c))
    weight_in.wait()

    own_lanes = pl.ds(pl.multiple_of(y * R, R), R)
    other_lanes = pl.ds(pl.multiple_of((1 - y) * R, R), R)

    def logits_of(k, lanes):
        at_k = slice(256 * k, 256 * (k + 1))
        lg[at_k, lanes] = nt(w[at_k, :], hx[lanes, 0:D])

    own_crossed, crossed = crossed, {}
    for k in range(4):
        logits_of(k, own_lanes)
        for kk in ((0, 4), (3, 5), (1, 7), (2, 6))[k]:
            for device, hh in zip(near_y, (h, 1 - h)):
                ticket = by_y[kk][0 if device is near_y[0] else 1]
                arrive(ticket, block(zs[kk], hh, 1 - y))
            cross(kk, 1 - y)

    ones = lax.broadcasted_iota(jnp.int32, (8, 128), 0) == lax.broadcasted_iota(jnp.int32, (8, 128), 1)
    ones = ones.astype(F32).astype(BF16)

    def marks(lanes):
        halves = nt(ones, hx[lanes, D:HX])
        return (halves[0:1] * 256.0 + halves[1:2]).astype(jnp.int32) - me_v * VD

    marked = marks(own_lanes)
    top = jnp.max(lg[:, own_lanes], axis=0, keepdims=True)

    def sums_of(k, carry):
        total, named = carry
        at_k = pl.ds(pl.multiple_of(k * 64, 64), 64)
        part = lg[at_k, own_lanes]
        code_at = lax.broadcasted_iota(jnp.int32, (64, R), 0) + k * 64
        named = named + jnp.sum(jnp.where(code_at == marked, part, 0.0), axis=0, keepdims=True)
        grown = jnp.exp(part - top)
        lg[at_k, own_lanes] = grown
        return total + jnp.sum(grown, axis=0, keepdims=True), named

    total, named = lax.fori_loop(
        0, VD // 64, sums_of, (jnp.zeros((1, R), F32), jnp.zeros((1, R), F32))
    )

    def fold(row):
        return jnp.concatenate([row[:, 128 * k : 128 * (k + 1)] for k in range(R // 128)], axis=0)

    def unfold(tile):
        return jnp.concatenate([tile[k : k + 1] for k in range(R // 128)], axis=1)

    def join(tops, totals, nameds):
        best = tops[0]
        for other_top in tops[1:]:
            best = jnp.maximum(best, other_top)
        total = sum(t * jnp.exp(m - best) for t, m in zip(totals, tops))
        return best, total, sum(nameds)

    def begin(triple, out_ref, in_ref, devices):
        out_ref[0:4], out_ref[4:8], out_ref[8:12] = triple
        out_ref[12:16] = jnp.zeros((4, 128), F32)
        return [send(out_ref, in_ref.at[k], device) for k, device in enumerate(devices)]

    def end(triple, in_ref, tickets):
        parts = [triple]
        for k, ticket in enumerate(tickets):
            arrive(ticket, in_ref.at[k])
            parts.append((in_ref[k, 0:4], in_ref[k, 4:8], in_ref[k, 8:12]))
        return join(*zip(*parts))

    triple = tuple(fold(row) for row in (top, total, named))
    tickets = begin(triple, st_mine, st_in, layer)
    for k in range(8):
        arrive(crossed[(0, 4, 3, 5, 1, 7, 2, 6)[k]], pair(zs[(0, 4, 3, 5, 1, 7, 2, 6)[k]], 1 - c, 1 - y))
    logits_of(0, other_lanes)
    logits_of(1, other_lanes)
    triple = end(triple, st_in, tickets)
    tickets = begin(triple, tot_mine, tot_in, column)
    logits_of(2, other_lanes)
    logits_of(3, other_lanes)
    other_marked = marks(other_lanes)
    row_top, row_total, row_named = end(triple, tot_in, tickets)
    log_total = row_top + jnp.log(row_total)
    lt_mine[0:4] = log_total
    lt_mine[4:8] = jnp.zeros((4, 128), F32)
    lt_ticket = send(lt_mine, lt_in, near_y[0])

    factor = LOSS_SCALE * jnp.exp(top - unfold(log_total))

    def own_grads(k, _):
        at_k = pl.ds(pl.multiple_of(k * 128, 128), 128)
        code_at = lax.broadcasted_iota(jnp.int32, (128, R), 0) + k * 128
        grad = lg[at_k, own_lanes] * factor - jnp.where(code_at == marked, LOSS_SCALE, 0.0)
        gt[at_k, own_lanes] = grad.astype(BF16)
        g[:, at_k] = grad.T.astype(BF16)
        return 0

    lax.fori_loop(0, VD // 128, own_grads, 0)

    def core_rows(cc):
        return pl.ds(pl.multiple_of(cc * 256, 256), 256)

    def theirs(k, _):
        at_k = pl.ds(pl.multiple_of(k * 512, 512), 512)
        hd_out[:, at_k] = nn(g[core_rows(1 - c), :], w[:, at_k]).astype(BF16)
        return 0

    lax.fori_loop(0, D // 512, theirs, 0)
    d_ticket = send(hd_out, hd_in, other_c)

    arrive(lt_ticket, lt_in)
    other_total = unfold(lt_in[0:4])

    def other_grads(k, _):
        at_k = pl.ds(pl.multiple_of(k * 128, 128), 128)
        code_at = lax.broadcasted_iota(jnp.int32, (128, R), 0) + k * 128
        grad = jnp.exp(lg[at_k, other_lanes] - other_total)
        grad = LOSS_SCALE * (grad - jnp.where(code_at == other_marked, 1.0, 0.0))
        gt[at_k, other_lanes] = grad.astype(BF16)
        return 0

    lax.fori_loop(0, VD // 128, other_grads, 0)

    def part(chunk, xx):
        start, size = chunk
        at_s = pl.ds(pl.multiple_of((y * 4 + xx) * CW, CW), CW)
        return nn(gt[start : start + size, :], hx[:, at_s])

    def halves_of(chunk):
        start, size = chunk
        return slice(start, start + size // 2), slice(start + size // 2, start + size)

    a_tickets, lr_tickets = [], []
    for chunk in CHUNKS:
        start, size = chunk
        xs[0, start : start + size, :] = part(chunk, far_x).astype(BF16)
        a_tickets.append([
            send(xs.at[0, spot], xa_in.at[spot], at(xx=to))
            for spot, to in zip(halves_of(chunk), (right_x, left_x))
        ])

    arrive(d_ticket, hd_in)

    def ours(k, _):
        at_k = pl.ds(pl.multiple_of(k * 512, 512), 512)
        hacc[:, at_k] = nn(g[core_rows(c), :], w[:, at_k]) + hd_in[:, at_k].astype(F32)
        return 0

    lax.fori_loop(0, D // 512, ours, 0)

    def owner_rows(k, hh):
        return pl.ds(pl.multiple_of(zs[k] * 32 + hh * 16, 16), 16)

    h_tickets = []
    for first, last in GROUPS:
        for slot in range(first, last):
            yo[slot] = hacc[owner_rows(FAR[slot], 1 - h), :].astype(BF16)
        h_tickets.append(send(yo.at[first:last], yi.at[first:last], other_h))

    z_tickets = {}

    def along_z(group):
        first, last = GROUPS[group]
        arrive(h_tickets[group], yi.at[first:last])
        for slot in range(first, last):
            k = FAR[slot]
            if k:
                zo[slot] = (hacc[owner_rows(k, h), :] + yi[slot].astype(F32)).astype(BF16)
                z_tickets[slot] = send(zo.at[slot], zi.at[slot], at(zz=zs[k]))

    for k, chunk in enumerate(CHUNKS):
        start, size = chunk
        sides = []
        for side, (to, into) in enumerate(((right_x, xl_in), (left_x, xr_in))):
            value = part(chunk, to)
            spot = halves_of(chunk)[side]
            arrive(a_tickets[k][side], xa_in.at[spot])
            near = xa_in[spot, :].astype(F32)
            half = size // 2
            if side == 0:
                value = jnp.concatenate([value[:half] + near, value[half:]], axis=0)
            else:
                value = jnp.concatenate([value[:half], value[half:] + near], axis=0)
            xs[1 + side, start : start + size, :] = value.astype(BF16)
            sides.append(send(
                xs.at[1 + side, start : start + size], into.at[start : start + size], at(xx=to)
            ))
        lr_tickets.append(sides)
        along_z(k)

    loss_mine[0:4] = log_total - row_named
    lanes8 = lax.broadcasted_iota(jnp.int32, (4, 128), 1)
    sends = jnp.zeros((4, 128), F32)
    for j in range(NS):
        sends = jnp.where(lanes8 == j, counts[0, 0, j].astype(F32), sends)
    loss_mine[4:8] = sends
    loss_tickets = [send(loss_mine, loss_in.at[k], device) for k, device in enumerate(others)]

    for k, chunk in enumerate(CHUNKS):
        start, size = chunk
        spot = slice(start, start + size)
        value = part(chunk, x)
        arrive(lr_tickets[k][0], xl_in.at[spot])
        arrive(lr_tickets[k][1], xr_in.at[spot])
        value = value + xl_in[spot, :].astype(F32) + xr_in[spot, :].astype(F32)
        code_out[spot, :] = value.astype(BF16)

    own = hacc[owner_rows(0, h), :] + yi[7].astype(F32)
    for slot in range(7):
        arrive(z_tickets[slot], zi.at[slot])
        own = own + zi[slot].astype(F32)
    spread = position((2 * RD, RD), 1) == lax.broadcasted_iota(jnp.int32, (2 * RD, RD), 0)
    hid_out[...] = nn(spread.astype(F32).astype(BF16), own.astype(BF16)).astype(BF16)

    tiles = [loss_mine[...]]
    for k, ticket in enumerate(loss_tickets):
        arrive(ticket, loss_in.at[k])
        tiles.append(loss_in[k])
    lane1 = lax.broadcasted_iota(jnp.int32, (1, 128), 1)
    own_row = lax.broadcasted_iota(jnp.int32, (4, 128), 0) == (c * 2 + z // 4)
    rank = lane1 - (lax.rem(z, 4) * 32 + h * 16)
    in_block = (rank >= 0) & (rank < RD)
    slots = lax.broadcasted_iota(jnp.int32, (RD, 128), 0)
    got, before, losses = [], [], []
    for tile in tiles:
        row = tile[4:5]
        got.append(jnp.sum(jnp.where(lane1 == me_s, row, 0.0), axis=1, keepdims=True).astype(jnp.int32))
        before.append(jnp.sum(jnp.where(lane1 < me_s, row, 0.0), axis=1, keepdims=True).astype(jnp.int32))
        losses.append(jnp.sum(jnp.where(own_row, tile[0:4], 0.0), axis=0, keepdims=True))
    listed = jnp.zeros((RD, 128), F32)
    for k in range(NS):
        source = lax.rem(me_s + NS - k, NS)
        first = jnp.zeros((1, 1), jnp.int32)
        for j in range(NS):
            earlier = lax.rem(me_s + NS - j, NS) < source
            first = first + jnp.where(earlier, got[j], 0)
        offset = rank - before[k]
        live = in_block & (offset >= 0) & (offset < got[k])
        slot = jnp.where(live, first + offset, -1)
        listed = listed + jnp.where(slots == slot, losses[k], 0.0)
    loss_out[...] = listed

    for copy in sent:
        copy.wait_send()


def per_device(hidden, head_weight, targets, span_counts, send_counts):
    vmem, smem = pl.BlockSpec(memory_space=pltpu.VMEM), pl.BlockSpec(memory_space=pltpu.SMEM)
    copies = 160
    code_grad, hidden_grad, listed = pl.pallas_call(
        body,
        out_shape=(
            jax.ShapeDtypeStruct((VD, CW), BF16),
            jax.ShapeDtypeStruct((2 * RD, D), BF16),
            jax.ShapeDtypeStruct((RD, 128), F32),
        ),
        in_specs=[smem, smem, smem, vmem, pl.BlockSpec(memory_space=pl.ANY)],
        out_specs=(vmem, vmem, vmem),
        scratch_shapes=[
            pltpu.VMEM((VD, D), BF16),
            pltpu.VMEM((2 * R, HX), BF16),
            pltpu.VMEM((VD, 2 * R), F32),
            pltpu.VMEM((VD, 2 * R), BF16),
            pltpu.VMEM((R, VD), BF16),
            pltpu.VMEM((16, 128), F32),
            pltpu.VMEM((3, 16, 128), F32),
            pltpu.VMEM((16, 128), F32),
            pltpu.VMEM((7, 16, 128), F32),
            pltpu.VMEM((8, 128), F32),
            pltpu.VMEM((8, 128), F32),
            pltpu.VMEM((8, 128), F32),
            pltpu.VMEM((7, 8, 128), F32),
            pltpu.VMEM((3, VD, CW), BF16),
            pltpu.VMEM((VD, CW), BF16),
            pltpu.VMEM((VD, CW), BF16),
            pltpu.VMEM((VD, CW), BF16),
            pltpu.VMEM((256, D), BF16),
            pltpu.VMEM((256, D), BF16),
            pltpu.VMEM((256, D), F32),
            pltpu.VMEM((8, RD, D), BF16),
            pltpu.VMEM((8, RD, D), BF16),
            pltpu.VMEM((7, RD, D), BF16),
            pltpu.VMEM((7, RD, D), BF16),
            pltpu.SemaphoreType.DMA((copies,)),
            pltpu.SemaphoreType.DMA((copies,)),
            pltpu.SemaphoreType.DMA,
        ],
        compiler_params=pltpu.CompilerParams(
            collective_id=0, has_side_effects=True, vmem_limit_bytes=56 * 1024 * 1024
        ),
        name="head",
    )(span_counts, send_counts, targets, hidden, head_weight)
    return (
        jnp.sum(listed, axis=1).reshape(1, 1, RD),
        hidden_grad.reshape(hidden.shape),
        code_grad,
    )


def solution(mesh):
    in_specs = (
        P("seq", "vocab", None, None, None),
        P("vocab", None),
        P("seq", "vocab", None, None),
        P("seq", "vocab", None),
        P("seq", "vocab", None),
    )
    out_specs = (P("seq", "vocab", None), P("seq", "vocab", None, None, None), P("vocab", "seq"))
    return jax.shard_map(
        per_device, mesh=mesh, in_specs=in_specs, out_specs=out_specs, check_vma=False
    )
```

```python
import itertools

import jax
import jax.numpy as jnp
from jax import lax
from jax.experimental import pallas as pl
from jax.experimental.pallas import tpu as pltpu
from jax.sharding import PartitionSpec as P

LOSS_SCALE = 4.0
D = 2048
VD = 1024
RD = 16
NV = 32
R = RD * NV
NS = 8
CW = D // NS
HX = D + 128
CHUNKS = [(256 * k, 256) for k in range(4)]
FAR = (4, 3, 5, 2, 6)
GROUPS = ((0, 1), (1, 3), (3, 5))
F32, BF16 = jnp.float32, jnp.bfloat16
MESH = pl.DeviceIdType.MESH


def nt(a, b):
    return lax.dot_general(a, b, (((1,), (1,)), ((), ())), preferred_element_type=F32)


def nn(a, b):
    return jnp.dot(a, b, preferred_element_type=F32)


def body(
    spans, counts, targets, hidden_at, weight,
    code_out, hid_out, loss_out,
    w, hx, lg, gt, g,
    st_mine, st_in, tot_mine, tot_in, lt_mine, lt_in, loss_mine, loss_in,
    xs, xa_in, xl_in, xr_in,
    hd_out, hd_in, hacc, yo, yi, zo, zi, zp_out, zp_in,
    hidden, ssem, rsem, wsem,
):
    me_s, me_v = lax.axis_index("seq"), lax.axis_index("vocab")
    x, y = lax.rem(me_s, 4), me_s // 4
    z, h, c = me_v // 4, lax.rem(me_v // 2, 2), lax.rem(me_v, 2)
    ids = itertools.count()
    sent = []

    def at(xx=None, yy=None, zz=None, hh=None, cc=None):
        xx, yy, zz, hh, cc = (
            mine if other is None else other
            for other, mine in ((xx, x), (yy, y), (zz, z), (hh, h), (cc, c))
        )
        return {"seq": yy * 4 + xx, "vocab": zz * 4 + hh * 2 + cc}

    def send(src, dst, device):
        i = next(ids)
        copy = pltpu.make_async_remote_copy(
            src_ref=src, dst_ref=dst, send_sem=ssem.at[i], recv_sem=rsem.at[i],
            device_id=device, device_id_type=MESH,
        )
        copy.start()
        sent.append(copy)
        return i, device

    def arrive(ticket, where):
        i, device = ticket
        pltpu.make_async_remote_copy(
            src_ref=where, dst_ref=where, send_sem=ssem.at[i], recv_sem=rsem.at[i],
            device_id=device, device_id_type=MESH,
        ).wait_recv()

    right_x, left_x, far_x = (lax.rem(x + k, 4) for k in (1, 3, 2))
    zs = [lax.rem(z + k, 8) for k in range(8)]
    other_c, other_h = at(cc=1 - c), at(hh=1 - h)
    near_y = [at(yy=1 - y), at(yy=1 - y, hh=1 - h)]
    layer = [other_c, other_h, at(hh=1 - h, cc=1 - c)]
    column = [at(zz=zs[k]) for k in range(1, 8)]
    others = [
        {"seq": lax.rem(me_s + k, NS), "vocab": me_v} for k in range(1, NS)
    ]
    peers = layer + column + others + near_y[1:]

    barrier = pltpu.get_barrier_semaphore()
    for device in peers:
        pl.semaphore_signal(barrier, inc=1, device_id=device, device_id_type=MESH)
    hidden_in = pltpu.make_async_copy(hidden_at, hidden, wsem.at[0])
    hidden_in.start()
    weight_in = pltpu.make_async_copy(weight, w, wsem.at[1])
    weight_in.start()

    s0 = spans[0, 0, 0]

    def position(shape, axis):
        rank = lax.broadcasted_iota(jnp.int32, shape, axis)
        return jnp.where(rank < s0, RD - s0 + rank, RD + rank)

    pick = position((RD, 2 * RD), 0) == lax.broadcasted_iota(jnp.int32, (RD, 2 * RD), 1)
    hidden_in.wait()
    packed = nn(pick.astype(F32).astype(BF16), hidden[0, 0].reshape(2 * RD, D)).astype(BF16)
    place = position((RD, 128), 0)
    code = jnp.zeros((RD, 128), jnp.int32)
    for q in range(2):
        for p in range(RD):
            code = jnp.where(place == q * RD + p, targets[0, 0, q, p], code)
    lane = lax.broadcasted_iota(jnp.int32, (RD, 128), 1)
    extra = jnp.where(lane == 0, code // 256, jnp.where(lane == 1, lax.rem(code, 256), 0))

    def rows(zz, hh, cc, yy, size=16):
        return pl.ds(pl.multiple_of(yy * R + cc * 256 + zz * 32 + hh * 16, 16), size)

    def block(zz, hh, yy=y):
        return hx.at[rows(zz, hh, c, yy)]

    def pair(zz, cc=c, yy=y):
        return hx.at[rows(zz, 0, cc, yy, 32)]

    mine = block(z, h)
    hx[rows(z, h, c, y), 0:D] = packed
    hx[rows(z, h, c, y), D:HX] = extra.astype(F32).astype(BF16)
    pl.semaphore_wait(barrier, len(peers))

    up, down = at(zz=zs[1]), at(zz=zs[7])
    by_z, by_y, by_h = {}, {}, {}
    crossed = {}

    def cross(k, yy=y):
        crossed[k] = send(pair(zs[k], c, yy), pair(zs[k], c, yy), other_c)

    def spread_y(k):
        here = block(zs[k], h)
        by_y[k] = [send(here, here, device) for device in near_y]

    by_h[0] = send(mine, mine, other_h)
    for k in (4, 3, 5, 1, 7, 2, 6):
        by_z[(8 - k) % 8] = send(mine, mine, at(zz=zs[k]))
    spread_y(0)
    arrive(by_h[0], block(z, 1 - h))
    other = block(z, 1 - h)
    ups, downs = send(other, other, up), send(other, other, down)
    cross(0)
    for k in (4, 3, 5):
        here = block(zs[k], h)
        arrive(by_z[k], here)
        by_h[k] = send(here, here, other_h)
        spread_y(k)
    for k in (1, 7):
        arrive(by_z[k], block(zs[k], h))
        spread_y(k)
    here = block(zs[7], 1 - h)
    arrive(ups, here)
    ups = send(here, here, up)
    cross(7)
    here = block(zs[1], 1 - h)
    arrive(downs, here)
    downs = send(here, here, down)
    cross(1)
    for k in (2, 6):
        arrive(by_z[k], block(zs[k], h))
        spread_y(k)
    for k in (4, 3, 5):
        arrive(by_h[k], block(zs[k], 1 - h))
        cross(k)
    arrive(ups, block(zs[6], 1 - h))
    cross(6)
    arrive(downs, block(zs[2], 1 - h))
    cross(2)
    for k in (0, 7, 1, 4, 3, 5, 6, 2):
        arrive(crossed[k], pair(zs[k], 1 - c))
    weight_in.wait()

    own_lanes = pl.ds(pl.multiple_of(y * R, R), R)
    other_lanes = pl.ds(pl.multiple_of((1 - y) * R, R), R)

    def logits_of(k, lanes):
        at_k = slice(256 * k, 256 * (k + 1))
        lg[at_k, lanes] = nt(w[at_k, :], hx[lanes, 0:D])

    own_crossed, crossed = crossed, {}
    for k in range(4):
        logits_of(k, own_lanes)
        for kk in ((0, 1), (7, 2), (6, 4), (3, 5))[k]:
            for device, hh in zip(near_y, (h, 1 - h)):
                ticket = by_y[kk][0 if device is near_y[0] else 1]
                arrive(ticket, block(zs[kk], hh, 1 - y))
            cross(kk, 1 - y)

    ones = lax.broadcasted_iota(jnp.int32, (8, 128), 0) == lax.broadcasted_iota(jnp.int32, (8, 128), 1)
    ones = ones.astype(F32).astype(BF16)

    def marks(lanes):
        halves = nt(ones, hx[lanes, D:HX])
        return (halves[0:1] * 256.0 + halves[1:2]).astype(jnp.int32) - me_v * VD

    marked = marks(own_lanes)
    top = jnp.max(lg[:, own_lanes], axis=0, keepdims=True)

    def sums_of(k, carry):
        total, named = carry
        at_k = pl.ds(pl.multiple_of(k * 64, 64), 64)
        part = lg[at_k, own_lanes]
        code_at = lax.broadcasted_iota(jnp.int32, (64, R), 0) + k * 64
        named = named + jnp.sum(jnp.where(code_at == marked, part, 0.0), axis=0, keepdims=True)
        grown = jnp.exp(part - top)
        lg[at_k, own_lanes] = grown
        return total + jnp.sum(grown, axis=0, keepdims=True), named

    total, named = lax.fori_loop(
        0, VD // 64, sums_of, (jnp.zeros((1, R), F32), jnp.zeros((1, R), F32))
    )

    def fold(row):
        return jnp.concatenate([row[:, 128 * k : 128 * (k + 1)] for k in range(R // 128)], axis=0)

    def unfold(tile):
        return jnp.concatenate([tile[k : k + 1] for k in range(R // 128)], axis=1)

    def join(tops, totals, nameds):
        best = tops[0]
        for other_top in tops[1:]:
            best = jnp.maximum(best, other_top)
        total = sum(t * jnp.exp(m - best) for t, m in zip(totals, tops))
        return best, total, sum(nameds)

    def begin(triple, out_ref, in_ref, devices):
        out_ref[0:4], out_ref[4:8], out_ref[8:12] = triple
        out_ref[12:16] = jnp.zeros((4, 128), F32)
        return [send(out_ref, in_ref.at[k], device) for k, device in enumerate(devices)]

    def end(triple, in_ref, tickets):
        parts = [triple]
        for k, ticket in enumerate(tickets):
            arrive(ticket, in_ref.at[k])
            parts.append((in_ref[k, 0:4], in_ref[k, 4:8], in_ref[k, 8:12]))
        return join(*zip(*parts))

    triple = tuple(fold(row) for row in (top, total, named))
    tickets = begin(triple, st_mine, st_in, layer)
    for k in range(8):
        arrive(crossed[k], pair(zs[k], 1 - c, 1 - y))
    logits_of(0, other_lanes)
    logits_of(1, other_lanes)
    triple = end(triple, st_in, tickets)
    tickets = begin(triple, tot_mine, tot_in, column)
    logits_of(2, other_lanes)
    logits_of(3, other_lanes)
    other_marked = marks(other_lanes)
    row_top, row_total, row_named = end(triple, tot_in, tickets)
    log_total = row_top + jnp.log(row_total)
    lt_mine[0:4] = log_total
    lt_mine[4:8] = jnp.zeros((4, 128), F32)
    lt_ticket = send(lt_mine, lt_in, near_y[0])

    factor = LOSS_SCALE * jnp.exp(top - unfold(log_total))

    def own_grads(k, _):
        at_k = pl.ds(pl.multiple_of(k * 128, 128), 128)
        code_at = lax.broadcasted_iota(jnp.int32, (128, R), 0) + k * 128
        grad = lg[at_k, own_lanes] * factor - jnp.where(code_at == marked, LOSS_SCALE, 0.0)
        gt[at_k, own_lanes] = grad.astype(BF16)
        g[:, at_k] = grad.T.astype(BF16)
        return 0

    lax.fori_loop(0, VD // 128, own_grads, 0)

    def core_rows(cc):
        return pl.ds(pl.multiple_of(cc * 256, 256), 256)

    def theirs(k, _):
        at_k = pl.ds(pl.multiple_of(k * 512, 512), 512)
        hd_out[:, at_k] = nn(g[core_rows(1 - c), :], w[:, at_k]).astype(BF16)
        return 0

    lax.fori_loop(0, D // 512, theirs, 0)
    d_ticket = send(hd_out, hd_in, other_c)

    arrive(lt_ticket, lt_in)
    other_total = unfold(lt_in[0:4])

    def other_grads(k, _):
        at_k = pl.ds(pl.multiple_of(k * 128, 128), 128)
        code_at = lax.broadcasted_iota(jnp.int32, (128, R), 0) + k * 128
        grad = jnp.exp(lg[at_k, other_lanes] - other_total)
        grad = LOSS_SCALE * (grad - jnp.where(code_at == other_marked, 1.0, 0.0))
        gt[at_k, other_lanes] = grad.astype(BF16)
        return 0

    lax.fori_loop(0, VD // 128, other_grads, 0)

    def part(chunk, xx):
        start, size = chunk
        at_s = pl.ds(pl.multiple_of((y * 4 + xx) * CW, CW), CW)
        return nn(gt[start : start + size, :], hx[:, at_s])

    def halves_of(chunk):
        start, size = chunk
        return slice(start, start + size // 2), slice(start + size // 2, start + size)

    a_tickets, lr_tickets = [], []
    for chunk in CHUNKS:
        start, size = chunk
        xs[0, start : start + size, :] = part(chunk, far_x).astype(BF16)
        a_tickets.append([
            send(xs.at[0, spot], xa_in.at[spot], at(xx=to))
            for spot, to in zip(halves_of(chunk), (right_x, left_x))
        ])

    arrive(d_ticket, hd_in)

    def ours(k, _):
        at_k = pl.ds(pl.multiple_of(k * 512, 512), 512)
        hacc[:, at_k] = nn(g[core_rows(c), :], w[:, at_k]) + hd_in[:, at_k].astype(F32)
        return 0

    lax.fori_loop(0, D // 512, ours, 0)

    def owner_rows(k, hh):
        return pl.ds(pl.multiple_of(zs[k] * 32 + hh * 16, 16), 16)

    p_tickets = []
    for i, k in enumerate((1, 7)):
        zp_out[i] = hacc[pl.ds(pl.multiple_of(zs[k] * 32, 32), 32), :].astype(BF16)
        p_tickets.append(send(zp_out.at[i], zp_in.at[i], at(zz=zs[k])))
    h_tickets = []
    for first, last in GROUPS:
        for slot in range(first, last):
            yo[slot] = hacc[owner_rows(FAR[slot], 1 - h), :].astype(BF16)
        h_tickets.append(send(yo.at[first:last], yi.at[first:last], other_h))

    z_tickets = {}

    def along_z(group):
        first, last = GROUPS[group]
        arrive(h_tickets[group], yi.at[first:last])
        for slot in range(first, last):
            k = FAR[slot]
            zo[slot] = (hacc[owner_rows(k, h), :] + yi[slot].astype(F32)).astype(BF16)
            z_tickets[slot] = send(zo.at[slot], zi.at[slot], at(zz=zs[k]))

    def near_sum(hh):
        at_h = pl.ds(pl.multiple_of(hh * 16, 16), 16)
        return hacc[owner_rows(0, hh), :] + zp_in[0, at_h, :].astype(F32) + zp_in[1, at_h, :].astype(F32)

    for k, chunk in enumerate(CHUNKS):
        start, size = chunk
        sides = []
        for side, (to, into) in enumerate(((right_x, xl_in), (left_x, xr_in))):
            value = part(chunk, to)
            spot = halves_of(chunk)[side]
            arrive(a_tickets[k][side], xa_in.at[spot])
            near = xa_in[spot, :].astype(F32)
            half = size // 2
            if side == 0:
                value = jnp.concatenate([value[:half] + near, value[half:]], axis=0)
            else:
                value = jnp.concatenate([value[:half], value[half:] + near], axis=0)
            xs[1 + side, start : start + size, :] = value.astype(BF16)
            sides.append(send(
                xs.at[1 + side, start : start + size], into.at[start : start + size], at(xx=to)
            ))
        lr_tickets.append(sides)
        if k < 3:
            along_z(k)
        if k == 1:
            for i, ticket in enumerate(p_tickets):
                arrive(ticket, zp_in.at[i])
            yo[5] = near_sum(1 - h).astype(BF16)
            near_ticket = send(yo.at[5], yi.at[5], other_h)

    loss_mine[0:4] = log_total - row_named
    lanes8 = lax.broadcasted_iota(jnp.int32, (4, 128), 1)
    sends = jnp.zeros((4, 128), F32)
    for j in range(NS):
        sends = jnp.where(lanes8 == j, counts[0, 0, j].astype(F32), sends)
    loss_mine[4:8] = sends
    loss_tickets = [send(loss_mine, loss_in.at[k], device) for k, device in enumerate(others)]

    for k, chunk in enumerate(CHUNKS):
        start, size = chunk
        spot = slice(start, start + size)
        value = part(chunk, x)
        arrive(lr_tickets[k][0], xl_in.at[spot])
        arrive(lr_tickets[k][1], xr_in.at[spot])
        value = value + xl_in[spot, :].astype(F32) + xr_in[spot, :].astype(F32)
        code_out[spot, :] = value.astype(BF16)

    arrive(near_ticket, yi.at[5])
    own = near_sum(h) + yi[5].astype(F32)
    for slot in range(5):
        arrive(z_tickets[slot], zi.at[slot])
        own = own + zi[slot].astype(F32)
    spread = position((2 * RD, RD), 1) == lax.broadcasted_iota(jnp.int32, (2 * RD, RD), 0)
    hid_out[...] = nn(spread.astype(F32).astype(BF16), own.astype(BF16)).astype(BF16)

    tiles = [loss_mine[...]]
    for k, ticket in enumerate(loss_tickets):
        arrive(ticket, loss_in.at[k])
        tiles.append(loss_in[k])
    lane1 = lax.broadcasted_iota(jnp.int32, (1, 128), 1)
    own_row = lax.broadcasted_iota(jnp.int32, (4, 128), 0) == (c * 2 + z // 4)
    rank = lane1 - (lax.rem(z, 4) * 32 + h * 16)
    in_block = (rank >= 0) & (rank < RD)
    slots = lax.broadcasted_iota(jnp.int32, (RD, 128), 0)
    got, before, losses = [], [], []
    for tile in tiles:
        row = tile[4:5]
        got.append(jnp.sum(jnp.where(lane1 == me_s, row, 0.0), axis=1, keepdims=True).astype(jnp.int32))
        before.append(jnp.sum(jnp.where(lane1 < me_s, row, 0.0), axis=1, keepdims=True).astype(jnp.int32))
        losses.append(jnp.sum(jnp.where(own_row, tile[0:4], 0.0), axis=0, keepdims=True))
    listed = jnp.zeros((RD, 128), F32)
    for k in range(NS):
        source = lax.rem(me_s + NS - k, NS)
        first = jnp.zeros((1, 1), jnp.int32)
        for j in range(NS):
            earlier = lax.rem(me_s + NS - j, NS) < source
            first = first + jnp.where(earlier, got[j], 0)
        offset = rank - before[k]
        live = in_block & (offset >= 0) & (offset < got[k])
        slot = jnp.where(live, first + offset, -1)
        listed = listed + jnp.where(slots == slot, losses[k], 0.0)
    turned = jnp.concatenate([listed, jnp.zeros((128 - RD, 128), F32)], axis=0).T
    loss_out[0] = jnp.sum(turned, axis=0, keepdims=True)[:, 0:RD]

    for copy in sent:
        copy.wait_send()


def per_device(hidden, head_weight, targets, span_counts, send_counts):
    vmem, smem = pl.BlockSpec(memory_space=pltpu.VMEM), pl.BlockSpec(memory_space=pltpu.SMEM)
    copies = 160
    code_grad, hidden_grad, listed = pl.pallas_call(
        body,
        out_shape=(
            pltpu.VMEM((VD, CW), BF16),
            pltpu.VMEM((2 * RD, D), BF16),
            pltpu.VMEM((1, 1, RD), F32),
        ),
        in_specs=[smem, smem, smem, pl.BlockSpec(memory_space=pl.ANY), pl.BlockSpec(memory_space=pl.ANY)],
        out_specs=(vmem, vmem, vmem),
        scratch_shapes=[
            pltpu.VMEM((VD, D), BF16),
            pltpu.VMEM((2 * R, HX), BF16),
            pltpu.VMEM((VD, 2 * R), F32),
            pltpu.VMEM((VD, 2 * R), BF16),
            pltpu.VMEM((R, VD), BF16),
            pltpu.VMEM((16, 128), F32),
            pltpu.VMEM((3, 16, 128), F32),
            pltpu.VMEM((16, 128), F32),
            pltpu.VMEM((7, 16, 128), F32),
            pltpu.VMEM((8, 128), F32),
            pltpu.VMEM((8, 128), F32),
            pltpu.VMEM((8, 128), F32),
            pltpu.VMEM((7, 8, 128), F32),
            pltpu.VMEM((3, VD, CW), BF16),
            pltpu.VMEM((VD, CW), BF16),
            pltpu.VMEM((VD, CW), BF16),
            pltpu.VMEM((VD, CW), BF16),
            pltpu.VMEM((256, D), BF16),
            pltpu.VMEM((256, D), BF16),
            pltpu.VMEM((256, D), F32),
            pltpu.VMEM((6, RD, D), BF16),
            pltpu.VMEM((6, RD, D), BF16),
            pltpu.VMEM((5, RD, D), BF16),
            pltpu.VMEM((5, RD, D), BF16),
            pltpu.VMEM((2, 2 * RD, D), BF16),
            pltpu.VMEM((2, 2 * RD, D), BF16),
            pltpu.VMEM((1, 1, 2, RD, D), BF16),
            pltpu.SemaphoreType.DMA((copies,)),
            pltpu.SemaphoreType.DMA((copies,)),
            pltpu.SemaphoreType.DMA((2,)),
        ],
        compiler_params=pltpu.CompilerParams(
            collective_id=0, has_side_effects=True, vmem_limit_bytes=56 * 1024 * 1024
        ),
        name="head",
    )(span_counts, send_counts, targets, hidden, head_weight)
    code_grad, hidden_grad, losses = pl.pallas_call(
        hand_over,
        out_shape=(
            jax.ShapeDtypeStruct((VD, CW), BF16),
            jax.ShapeDtypeStruct((2 * RD, D), BF16),
            jax.ShapeDtypeStruct((1, 1, RD), F32),
        ),
        in_specs=[vmem] * 3,
        out_specs=(vmem,) * 3,
        name="hand_over",
    )(*(pltpu.with_memory_space_constraint(a, pltpu.VMEM) for a in (code_grad, hidden_grad, listed)))
    return losses, hidden_grad.reshape(hidden.shape), code_grad


def hand_over(code_in, hid_in, loss_in, code_out, hid_out, loss_out):
    code_out[...] = code_in[...]
    hid_out[...] = hid_in[...]
    loss_out[...] = loss_in[...]


def solution(mesh):
    in_specs = (
        P("seq", "vocab", None, None, None),
        P("vocab", None),
        P("seq", "vocab", None, None),
        P("seq", "vocab", None),
        P("seq", "vocab", None),
    )
    out_specs = (P("seq", "vocab", None), P("seq", "vocab", None, None, None), P("vocab", "seq"))
    return jax.shard_map(
        per_device, mesh=mesh, in_specs=in_specs, out_specs=out_specs, check_vma=False
    )
```

```python
import itertools

import jax
import jax.numpy as jnp
from jax import lax
from jax.experimental import pallas as pl
from jax.experimental.pallas import tpu as pltpu
from jax.sharding import PartitionSpec as P

LOSS_SCALE = 4.0
D = 2048
VD = 1024
RD = 16
NV = 32
R = RD * NV
NS = 8
CW = D // NS
HX = D + 128
CHUNKS = [(256 * k, 256) for k in range(4)]
FAR = (4, 3, 5, 2, 6)
GROUPS = ((0, 1), (1, 3), (3, 5))
F32, BF16 = jnp.float32, jnp.bfloat16
MESH = pl.DeviceIdType.MESH


def nt(a, b):
    return lax.dot_general(a, b, (((1,), (1,)), ((), ())), preferred_element_type=F32)


def nn(a, b):
    return jnp.dot(a, b, preferred_element_type=F32)


def body(
    spans, counts, targets, hidden_at, weight,
    code_out, hid_out, loss_out,
    w, hx, lg, gt, g,
    fc, st_mine, st_in, tot_mine, tot_in, loss_mine, loss_in,
    xs, xa_in, xl_in, xr_in,
    x_own, code_own, ha, hd_out, hd_in, hacc, yo, yi, zo, zi, zp_out, zp_in,
    hidden, ssem, rsem, wsem,
):
    me_s, me_v = lax.axis_index("seq"), lax.axis_index("vocab")
    x, y = lax.rem(me_s, 4), me_s // 4
    z, h, c = me_v // 4, lax.rem(me_v // 2, 2), lax.rem(me_v, 2)
    ids = itertools.count()
    sent = []

    def at(xx=None, yy=None, zz=None, hh=None, cc=None):
        xx, yy, zz, hh, cc = (
            mine if other is None else other
            for other, mine in ((xx, x), (yy, y), (zz, z), (hh, h), (cc, c))
        )
        return {"seq": yy * 4 + xx, "vocab": zz * 4 + hh * 2 + cc}

    def send(src, dst, device):
        i = next(ids)
        copy = pltpu.make_async_remote_copy(
            src_ref=src, dst_ref=dst, send_sem=ssem.at[i], recv_sem=rsem.at[i],
            device_id=device, device_id_type=MESH,
        )
        copy.start()
        sent.append(copy)
        return i, device

    def arrive(ticket, where):
        i, device = ticket
        pltpu.make_async_remote_copy(
            src_ref=where, dst_ref=where, send_sem=ssem.at[i], recv_sem=rsem.at[i],
            device_id=device, device_id_type=MESH,
        ).wait_recv()

    right_x, left_x, far_x = (lax.rem(x + k, 4) for k in (1, 3, 2))
    zs = [lax.rem(z + k, 8) for k in range(8)]
    other_c, other_h = at(cc=1 - c), at(hh=1 - h)
    near_y = [at(yy=1 - y), at(yy=1 - y, hh=1 - h)]
    layer = [other_c, other_h, at(hh=1 - h, cc=1 - c)]
    column = [at(zz=zs[k]) for k in (4, 3, 5, 2, 6, 1, 7)]
    others = [
        {"seq": lax.rem(me_s + k, NS), "vocab": me_v} for k in range(1, NS)
    ]
    across = [at(yy=1 - y, zz=zs[k]) for k in (4, 3, 5, 2, 6, 1, 7, 0)]
    peers = layer + column + others + near_y[1:] + across[:7]

    hidden_in = pltpu.make_async_copy(hidden_at, hidden, wsem.at[0])
    hidden_in.start()
    barrier = pltpu.get_barrier_semaphore()
    for device in peers:
        pl.semaphore_signal(barrier, inc=1, device_id=device, device_id_type=MESH)
    weight_in = pltpu.make_async_copy(weight, w, wsem.at[1])
    weight_in.start()

    s0 = spans[0, 0, 0]

    def position(shape, axis):
        rank = lax.broadcasted_iota(jnp.int32, shape, axis)
        return jnp.where(rank < s0, RD - s0 + rank, RD + rank)

    pick = position((RD, 2 * RD), 0) == lax.broadcasted_iota(jnp.int32, (RD, 2 * RD), 1)
    hidden_in.wait()
    packed = nn(pick.astype(F32).astype(BF16), hidden[0, 0].reshape(2 * RD, D)).astype(BF16)
    place = position((RD, 128), 0)
    code = jnp.zeros((RD, 128), jnp.int32)
    for q in range(2):
        for p in range(RD):
            code = jnp.where(place == q * RD + p, targets[0, 0, q, p], code)
    lane = lax.broadcasted_iota(jnp.int32, (RD, 128), 1)
    extra = jnp.where(lane == 0, code // 256, jnp.where(lane == 1, lax.rem(code, 256), 0))

    def rows(zz, hh, cc, yy, size=16):
        return pl.ds(pl.multiple_of(yy * R + cc * 256 + zz * 32 + hh * 16, 16), size)

    def block(zz, hh, yy=y):
        return hx.at[rows(zz, hh, c, yy)]

    def pair(zz, cc=c, yy=y):
        return hx.at[rows(zz, 0, cc, yy, 32)]

    mine = block(z, h)
    hx[rows(z, h, c, y), 0:D] = packed
    hx[rows(z, h, c, y), D:HX] = extra.astype(F32).astype(BF16)
    pl.semaphore_wait(barrier, len(peers))

    up, down = at(zz=zs[1]), at(zz=zs[7])
    by_z, by_y, by_h = {}, {}, {}
    crossed = {}

    def cross(k, yy=y):
        crossed[k] = send(pair(zs[k], c, yy), pair(zs[k], c, yy), other_c)

    def spread_y(k):
        here = block(zs[k], h)
        by_y[k] = [send(here, here, device) for device in near_y]

    by_h[0] = send(mine, mine, other_h)
    for k in (4, 3, 5, 1, 7, 2, 6):
        by_z[(8 - k) % 8] = send(mine, mine, at(zz=zs[k]))
    spread_y(0)
    arrive(by_h[0], block(z, 1 - h))
    other = block(z, 1 - h)
    ups, downs = send(other, other, up), send(other, other, down)
    cross(0)
    for k in (4, 3, 5):
        here = block(zs[k], h)
        arrive(by_z[k], here)
        by_h[k] = send(here, here, other_h)
        spread_y(k)
    for k in (1, 7):
        arrive(by_z[k], block(zs[k], h))
        spread_y(k)
    here = block(zs[7], 1 - h)
    arrive(ups, here)
    ups = send(here, here, up)
    cross(7)
    here = block(zs[1], 1 - h)
    arrive(downs, here)
    downs = send(here, here, down)
    cross(1)
    for k in (2, 6):
        arrive(by_z[k], block(zs[k], h))
        spread_y(k)
    for k in (4, 3, 5):
        arrive(by_h[k], block(zs[k], 1 - h))
        cross(k)
    arrive(ups, block(zs[6], 1 - h))
    cross(6)
    arrive(downs, block(zs[2], 1 - h))
    cross(2)
    for k in (0, 7, 1, 4, 3, 5, 6, 2):
        arrive(crossed[k], pair(zs[k], 1 - c))
    weight_in.wait()

    own_lanes = pl.ds(pl.multiple_of(y * R, R), R)
    other_lanes = pl.ds(pl.multiple_of((1 - y) * R, R), R)

    def logits_of(k, lanes):
        at_k = slice(512 * k, 512 * (k + 1))
        lg[at_k, lanes] = nt(w[at_k, :], hx[lanes, 0:D])

    crossed = {}

    def take_other(k):
        for ticket, hh in zip(by_y[k], (h, 1 - h)):
            arrive(ticket, block(zs[k], hh, 1 - y))
        cross(k, 1 - y)

    for k in range(2):
        logits_of(k, own_lanes)
        for kk in ((0, 1, 7), (2, 6))[k]:
            take_other(kk)

    ones = lax.broadcasted_iota(jnp.int32, (8, 128), 0) == lax.broadcasted_iota(jnp.int32, (8, 128), 1)
    ones = ones.astype(F32).astype(BF16)

    def marks(lanes):
        halves = nt(ones, hx[lanes, D:HX])
        return (halves[0:1] * 256.0 + halves[1:2]).astype(jnp.int32) - me_v * VD

    marked = marks(own_lanes)
    top = jnp.max(lg[:, own_lanes], axis=0, keepdims=True)

    def sums_of(k, carry):
        total, named, share = carry
        at_k = pl.ds(pl.multiple_of(k * 64, 64), 64)
        part = lg[at_k, own_lanes]
        hit = lax.broadcasted_iota(jnp.int32, (64, R), 0) + k * 64 == marked
        named = named + jnp.sum(jnp.where(hit, part, 0.0), axis=0, keepdims=True)
        grown = jnp.exp(part - top)
        lg[at_k, own_lanes] = grown
        share = share + jnp.sum(jnp.where(hit, grown, 0.0), axis=0, keepdims=True)
        return total + jnp.sum(grown, axis=0, keepdims=True), named, share

    total, named, share = lax.fori_loop(
        0, VD // 64, sums_of, tuple(jnp.zeros((1, R), F32) for _ in range(3))
    )

    def fold(row):
        return jnp.concatenate([row[:, 128 * k : 128 * (k + 1)] for k in range(R // 128)], axis=0)

    def unfold(tile):
        return jnp.concatenate([tile[k : k + 1] for k in range(R // 128)], axis=1)

    def join(tops, totals, nameds):
        best = tops[0]
        for other_top in tops[1:]:
            best = jnp.maximum(best, other_top)
        total = sum(t * jnp.exp(m - best) for t, m in zip(totals, tops))
        return best, total, sum(nameds)

    def begin(triple, out_ref, in_ref, devices):
        out_ref[0:4], out_ref[4:8], out_ref[8:12] = triple
        out_ref[12:16] = jnp.zeros((4, 128), F32)
        return [send(out_ref, in_ref.at[k], device) for k, device in enumerate(devices)]

    def end(triple, in_ref, tickets):
        parts = [triple]
        for k, ticket in enumerate(tickets):
            arrive(ticket, in_ref.at[k])
            parts.append((in_ref[k, 0:4], in_ref[k, 4:8], in_ref[k, 8:12]))
        return join(*zip(*parts))

    def core_lanes(cc):
        return pl.ds(pl.multiple_of(y * R + cc * 256, 256), 256)

    triple = tuple(fold(row) for row in (top, total, named))
    tickets = begin(triple, st_mine, st_in, layer)
    for k in (4, 3, 5):
        take_other(k)

    code_row = hx[core_lanes(1 - c), D:HX].astype(F32)
    code_row = code_row[:, 0:1] * 256.0 + code_row[:, 1:2] - (me_v * VD).astype(F32)
    their_marks = marks(core_lanes(1 - c))

    def unnamed(k, _):
        at_k = pl.ds(pl.multiple_of(k * 128, 128), 128)
        code_at = lax.broadcasted_iota(jnp.int32, (128, 256), 0) + k * 128
        grown = jnp.where(code_at == their_marks, 0.0, lg[at_k, core_lanes(1 - c)])
        g[0:256, at_k] = grown.T.astype(BF16)
        code_at = lax.broadcasted_iota(jnp.int32, (256, 128), 1) + k * 128
        g[256:512, at_k] = (code_at.astype(F32) == code_row).astype(F32).astype(BF16)
        return 0

    lax.fori_loop(0, VD // 128, unnamed, 0)
    for k in range(8):
        arrive(crossed[k], pair(zs[k], 1 - c, 1 - y))
    logits_of(0, other_lanes)
    triple = end(triple, st_in, tickets)
    tickets = begin(triple, tot_mine, tot_in, column + across)
    logits_of(1, other_lanes)
    other_marked = marks(other_lanes)

    def theirs(k, _):
        at_k = pl.ds(pl.multiple_of(k * 512, 512), 512)
        ha[:, at_k] = nn(g[...], w[:, at_k])
        return 0

    lax.fori_loop(0, D // 512, theirs, 0)
    row_top, row_total, row_named = end(triple, tot_in, tickets[:7])
    log_total = row_top + jnp.log(row_total)

    factor = LOSS_SCALE * jnp.exp(top - unfold(log_total))
    both = jnp.concatenate([factor, factor * share - LOSS_SCALE, jnp.zeros((126, R), F32)], axis=0)
    fc[...] = jnp.where(c == 0, both[:, 256:512], both[:, 0:256]).T

    d_tickets = []
    for k in range(4):
        at_k = slice(512 * k, 512 * (k + 1))
        hd_out[k] = (fc[:, 0:1] * ha[0:256, at_k] + fc[:, 1:2] * ha[256:512, at_k]).astype(BF16)
        d_tickets.append(send(hd_out.at[k], hd_in.at[k], other_c))

    other_parts = []
    for k, ticket in enumerate(tickets[7:]):
        arrive(ticket, tot_in.at[7 + k])
        other_parts.append((tot_in[7 + k, 0:4], tot_in[7 + k, 4:8], tot_in[7 + k, 8:12]))
    other_top, other_sum, _ = join(*zip(*other_parts))
    other_total = unfold(other_top + jnp.log(other_sum))

    def grads_of(k, _):
        at_k = pl.ds(pl.multiple_of(k * 128, 128), 128)
        code_at = lax.broadcasted_iota(jnp.int32, (128, R), 0) + k * 128
        grad = lg[at_k, own_lanes] * factor - jnp.where(code_at == marked, LOSS_SCALE, 0.0)
        gt[at_k, own_lanes] = grad.astype(BF16)
        g[0:256, at_k] = jnp.where(c == 0, grad[:, 0:256], grad[:, 256:512]).T.astype(BF16)
        grad = jnp.exp(lg[at_k, other_lanes] - other_total)
        grad = LOSS_SCALE * (grad - jnp.where(code_at == other_marked, 1.0, 0.0))
        gt[at_k, other_lanes] = grad.astype(BF16)
        return 0

    def part(chunk, xx):
        start, size = chunk
        at_s = pl.ds(pl.multiple_of((y * 4 + xx) * CW, CW), CW)
        return nn(gt[start : start + size, :], hx[:, at_s])

    def halves_of(chunk):
        start, size = chunk
        return slice(start, start + size // 2), slice(start + size // 2, start + size)

    a_tickets, lr_tickets = [], []
    for chunk in CHUNKS:
        start, size = chunk
        lax.fori_loop(start // 128, (start + size) // 128, grads_of, 0)
        xs[0, start : start + size, :] = part(chunk, far_x).astype(BF16)
        a_tickets.append([
            send(xs.at[0, spot], xa_in.at[spot], at(xx=to))
            for spot, to in zip(halves_of(chunk), (right_x, left_x))
        ])

    for k, ticket in enumerate(d_tickets):
        at_k = slice(512 * k, 512 * (k + 1))
        ours = nn(g[0:256, :], w[:, at_k])
        arrive(ticket, hd_in.at[k])
        hacc[:, at_k] = ours + hd_in[k].astype(F32)

    def owner_rows(k, hh):
        return pl.ds(pl.multiple_of(zs[k] * 32 + hh * 16, 16), 16)

    p_tickets = []
    for i, k in enumerate((1, 7)):
        zp_out[i] = hacc[pl.ds(pl.multiple_of(zs[k] * 32, 32), 32), :].astype(BF16)
        p_tickets.append(send(zp_out.at[i], zp_in.at[i], at(zz=zs[k])))
    h_tickets = []
    for first, last in GROUPS:
        for slot in range(first, last):
            yo[slot] = hacc[owner_rows(FAR[slot], 1 - h), :].astype(BF16)
        h_tickets.append(send(yo.at[first:last], yi.at[first:last], other_h))

    z_tickets = {}

    def along_z(group):
        first, last = GROUPS[group]
        arrive(h_tickets[group], yi.at[first:last])
        for slot in range(first, last):
            k = FAR[slot]
            zo[slot] = (hacc[owner_rows(k, h), :] + yi[slot].astype(F32)).astype(BF16)
            z_tickets[slot] = send(zo.at[slot], zi.at[slot], at(zz=zs[k]))

    def near_sum(hh):
        at_h = pl.ds(pl.multiple_of(hh * 16, 16), 16)
        return hacc[owner_rows(0, hh), :] + zp_in[0, at_h, :].astype(F32) + zp_in[1, at_h, :].astype(F32)

    sides = ((right_x, xl_in), (left_x, xr_in))
    for k, chunk in enumerate(CHUNKS):
        spots, half = halves_of(chunk), chunk[1] // 2
        tickets = []
        for side, (to, into) in enumerate(sides):
            value = part(chunk, to)
            joined, plain = value[:half], value[half:]
            if side:
                joined, plain = plain, joined
            x_own[side, half * k : half * (k + 1), :] = joined
            spot = spots[1 - side]
            xs[1 + side, spot, :] = plain.astype(BF16)
            tickets.append((send(xs.at[1 + side, spot], into.at[spot], at(xx=to)), into.at[spot]))
        lr_tickets.append(tickets)
        if k == 1:
            along_z(0)

    for k, chunk in enumerate(CHUNKS):
        spots, half = halves_of(chunk), chunk[1] // 2
        for side, (to, into) in enumerate(sides):
            spot = spots[side]
            arrive(a_tickets[k][side], xa_in.at[spot])
            value = x_own[side, half * k : half * (k + 1), :] + xa_in[spot, :].astype(F32)
            xs[1 + side, spot, :] = value.astype(BF16)
            ticket = send(xs.at[1 + side, spot], into.at[spot], at(xx=to))
            lr_tickets[k].append((ticket, into.at[spot]))
        if k == 0:
            along_z(1)
        if k == 1:
            for i, ticket in enumerate(p_tickets):
                arrive(ticket, zp_in.at[i])
            yo[5] = near_sum(1 - h).astype(BF16)
            near_ticket = send(yo.at[5], yi.at[5], other_h)
        if k == 2:
            along_z(2)

    loss_mine[0:4] = log_total - row_named
    lanes8 = lax.broadcasted_iota(jnp.int32, (4, 128), 1)
    sends = jnp.zeros((4, 128), F32)
    for j in range(NS):
        sends = jnp.where(lanes8 == j, counts[0, 0, j].astype(F32), sends)
    loss_mine[4:8] = sends
    loss_tickets = [send(loss_mine, loss_in.at[k], device) for k, device in enumerate(others)]

    for _ in range(len(sent) - 20):
        sent.pop(0).wait_send()

    for chunk in CHUNKS:
        start, size = chunk
        code_own[start : start + size, :] = part(chunk, x)
    tiles = [loss_mine[...]]
    for k, ticket in enumerate(loss_tickets):
        arrive(ticket, loss_in.at[k])
        tiles.append(loss_in[k])
    lane1 = lax.broadcasted_iota(jnp.int32, (1, 128), 1)
    own_row = lax.broadcasted_iota(jnp.int32, (4, 128), 0) == (c * 2 + z // 4)
    rank = lane1 - (lax.rem(z, 4) * 32 + h * 16)
    in_block = (rank >= 0) & (rank < RD)
    slots = lax.broadcasted_iota(jnp.int32, (RD, 128), 0)
    got, before, losses = [], [], []
    for tile in tiles:
        row = tile[4:5]
        got.append(jnp.sum(jnp.where(lane1 == me_s, row, 0.0), axis=1, keepdims=True).astype(jnp.int32))
        before.append(jnp.sum(jnp.where(lane1 < me_s, row, 0.0), axis=1, keepdims=True).astype(jnp.int32))
        losses.append(jnp.sum(jnp.where(own_row, tile[0:4], 0.0), axis=0, keepdims=True))
    listed = jnp.zeros((RD, 128), F32)
    for k in range(NS):
        source = lax.rem(me_s + NS - k, NS)
        first = jnp.zeros((1, 1), jnp.int32)
        for j in range(NS):
            earlier = lax.rem(me_s + NS - j, NS) < source
            first = first + jnp.where(earlier, got[j], 0)
        offset = rank - before[k]
        live = in_block & (offset >= 0) & (offset < got[k])
        slot = jnp.where(live, first + offset, -1)
        listed = listed + jnp.where(slots == slot, losses[k], 0.0)
    turned = jnp.concatenate([listed, jnp.zeros((128 - RD, 128), F32)], axis=0).T
    loss_out[0] = jnp.sum(turned, axis=0, keepdims=True)[:, 0:RD]

    for k, chunk in enumerate(CHUNKS):
        start, size = chunk
        spot = slice(start, start + size)
        value = code_own[spot, :]
        for ticket, where in lr_tickets[k]:
            arrive(ticket, where)
        value = value + xl_in[spot, :].astype(F32) + xr_in[spot, :].astype(F32)
        code_out[spot, :] = value.astype(BF16)

    arrive(near_ticket, yi.at[5])
    own = near_sum(h) + yi[5].astype(F32)
    for slot in range(5):
        arrive(z_tickets[slot], zi.at[slot])
        own = own + zi[slot].astype(F32)
    spread = position((2 * RD, RD), 1) == lax.broadcasted_iota(jnp.int32, (2 * RD, RD), 0)
    hid_out[...] = nn(spread.astype(F32).astype(BF16), own.astype(BF16)).astype(BF16)

    for copy in sent:
        copy.wait_send()


def per_device(hidden, head_weight, targets, span_counts, send_counts):
    vmem, smem = pl.BlockSpec(memory_space=pltpu.VMEM), pl.BlockSpec(memory_space=pltpu.SMEM)
    copies = 192
    code_grad, hidden_grad, listed = pl.pallas_call(
        body,
        out_shape=(
            pltpu.VMEM((VD, CW), BF16),
            pltpu.VMEM((2 * RD, D), BF16),
            pltpu.VMEM((1, 1, RD), F32),
        ),
        in_specs=[smem, smem, smem, pl.BlockSpec(memory_space=pl.ANY), pl.BlockSpec(memory_space=pl.ANY)],
        out_specs=(vmem, vmem, vmem),
        scratch_shapes=[
            pltpu.VMEM((VD, D), BF16),
            pltpu.VMEM((2 * R, HX), BF16),
            pltpu.VMEM((VD, 2 * R), F32),
            pltpu.VMEM((VD, 2 * R), BF16),
            pltpu.VMEM((512, VD), BF16),
            pltpu.VMEM((256, 128), F32),
            pltpu.VMEM((16, 128), F32),
            pltpu.VMEM((3, 16, 128), F32),
            pltpu.VMEM((16, 128), F32),
            pltpu.VMEM((15, 16, 128), F32),
            pltpu.VMEM((8, 128), F32),
            pltpu.VMEM((7, 8, 128), F32),
            pltpu.VMEM((3, VD, CW), BF16),
            pltpu.VMEM((VD, CW), BF16),
            pltpu.VMEM((VD, CW), BF16),
            pltpu.VMEM((VD, CW), BF16),
            pltpu.VMEM((2, VD // 2, CW), F32),
            pltpu.VMEM((VD, CW), F32),
            pltpu.VMEM((512, D), F32),
            pltpu.VMEM((4, 256, 512), BF16),
            pltpu.VMEM((4, 256, 512), BF16),
            pltpu.VMEM((256, D), F32),
            pltpu.VMEM((6, RD, D), BF16),
            pltpu.VMEM((6, RD, D), BF16),
            pltpu.VMEM((5, RD, D), BF16),
            pltpu.VMEM((5, RD, D), BF16),
            pltpu.VMEM((2, 2 * RD, D), BF16),
            pltpu.VMEM((2, 2 * RD, D), BF16),
            pltpu.VMEM((1, 1, 2, RD, D), BF16),
            pltpu.SemaphoreType.DMA((copies,)),
            pltpu.SemaphoreType.DMA((copies,)),
            pltpu.SemaphoreType.DMA((2,)),
        ],
        compiler_params=pltpu.CompilerParams(
            collective_id=0, has_side_effects=True, vmem_limit_bytes=56 * 1024 * 1024
        ),
        name="head",
    )(span_counts, send_counts, targets, hidden, head_weight)
    code_grad, hidden_grad, losses = pl.pallas_call(
        hand_over,
        out_shape=(
            jax.ShapeDtypeStruct((VD, CW), BF16),
            jax.ShapeDtypeStruct((2 * RD, D), BF16),
            jax.ShapeDtypeStruct((1, 1, RD), F32),
        ),
        in_specs=[vmem] * 3,
        out_specs=(vmem,) * 3,
        name="hand_over",
    )(*(pltpu.with_memory_space_constraint(a, pltpu.VMEM) for a in (code_grad, hidden_grad, listed)))
    return losses, hidden_grad.reshape(hidden.shape), code_grad


def hand_over(code_in, hid_in, loss_in, code_out, hid_out, loss_out):
    code_out[...] = code_in[...]
    hid_out[...] = hid_in[...]
    loss_out[...] = loss_in[...]


def solution(mesh):
    in_specs = (
        P("seq", "vocab", None, None, None),
        P("vocab", None),
        P("seq", "vocab", None, None),
        P("seq", "vocab", None),
        P("seq", "vocab", None),
    )
    out_specs = (P("seq", "vocab", None), P("seq", "vocab", None, None, None), P("vocab", "seq"))
    return jax.shard_map(
        per_device, mesh=mesh, in_specs=in_specs, out_specs=out_specs, check_vma=False
    )
```

```python
import itertools

import jax
import jax.numpy as jnp
from jax import lax
from jax.experimental import pallas as pl
from jax.experimental.pallas import tpu as pltpu
from jax.sharding import PartitionSpec as P

LOSS_SCALE = 4.0
D = 2048
VD = 1024
RD = 16
NV = 32
R = RD * NV
NS = 8
CW = D // NS
HX = D + 128
CHUNKS = [(256 * k, 256) for k in range(4)]
FAR = (4, 3, 5, 2, 6)
GROUPS = ((0, 1), (1, 3), (3, 5))
F32, BF16 = jnp.float32, jnp.bfloat16
MESH = pl.DeviceIdType.MESH


def nt(a, b):
    return lax.dot_general(a, b, (((1,), (1,)), ((), ())), preferred_element_type=F32)


def nn(a, b):
    return jnp.dot(a, b, preferred_element_type=F32)


def body(
    spans, counts, targets, hidden_at, weight,
    code_out, hid_out, loss_out,
    w, hx, lg, gt, g,
    fc, st_mine, st_in, tot_mine, tot_in, loss_mine, loss_in,
    xs, xa_in, xl_in, xr_in,
    x_own, code_own, ha, hd_out, hd_in, hacc, yo, yi, zo, zi, zp_out, zp_in,
    hidden, ssem, rsem, wsem,
):
    me_s, me_v = lax.axis_index("seq"), lax.axis_index("vocab")
    x, y = lax.rem(me_s, 4), me_s // 4
    z, h, c = me_v // 4, lax.rem(me_v // 2, 2), lax.rem(me_v, 2)
    ids = itertools.count()
    sent = []

    def at(xx=None, yy=None, zz=None, hh=None, cc=None):
        xx, yy, zz, hh, cc = (
            mine if other is None else other
            for other, mine in ((xx, x), (yy, y), (zz, z), (hh, h), (cc, c))
        )
        return {"seq": yy * 4 + xx, "vocab": zz * 4 + hh * 2 + cc}

    def send(src, dst, device):
        i = next(ids)
        copy = pltpu.make_async_remote_copy(
            src_ref=src, dst_ref=dst, send_sem=ssem.at[i], recv_sem=rsem.at[i],
            device_id=device, device_id_type=MESH,
        )
        copy.start()
        sent.append(copy)
        return i, device

    def arrive(ticket, where):
        i, device = ticket
        pltpu.make_async_remote_copy(
            src_ref=where, dst_ref=where, send_sem=ssem.at[i], recv_sem=rsem.at[i],
            device_id=device, device_id_type=MESH,
        ).wait_recv()

    right_x, left_x, far_x = (lax.rem(x + k, 4) for k in (1, 3, 2))
    zs = [lax.rem(z + k, 8) for k in range(8)]
    other_c, other_h = at(cc=1 - c), at(hh=1 - h)
    near_y = [at(yy=1 - y), at(yy=1 - y, hh=1 - h)]
    layer = [other_c, other_h, at(hh=1 - h, cc=1 - c)]
    column = [at(zz=zs[k]) for k in (4, 3, 5, 2, 6, 1, 7)]
    others = [
        {"seq": lax.rem(me_s + k, NS), "vocab": me_v} for k in range(1, NS)
    ]
    across = [at(yy=1 - y, zz=zs[k]) for k in (4, 3, 5, 2, 6, 1, 7, 0)]
    peers = layer + column + others + near_y[1:] + across[:7]

    hidden_in = pltpu.make_async_copy(hidden_at, hidden, wsem.at[0])
    hidden_in.start()
    barrier = pltpu.get_barrier_semaphore()
    for device in peers:
        pl.semaphore_signal(barrier, inc=1, device_id=device, device_id_type=MESH)
    weight_in = pltpu.make_async_copy(weight, w, wsem.at[1])
    weight_in.start()

    s0 = spans[0, 0, 0]

    def position(shape, axis):
        rank = lax.broadcasted_iota(jnp.int32, shape, axis)
        return jnp.where(rank < s0, RD - s0 + rank, RD + rank)

    pick = position((RD, 2 * RD), 0) == lax.broadcasted_iota(jnp.int32, (RD, 2 * RD), 1)
    hidden_in.wait()
    packed = nn(pick.astype(F32).astype(BF16), hidden[0, 0].reshape(2 * RD, D)).astype(BF16)
    place = position((RD, 128), 0)
    code = jnp.zeros((RD, 128), jnp.int32)
    for q in range(2):
        for p in range(RD):
            code = jnp.where(place == q * RD + p, targets[0, 0, q, p], code)
    lane = lax.broadcasted_iota(jnp.int32, (RD, 128), 1)
    extra = jnp.where(lane == 0, code // 256, jnp.where(lane == 1, lax.rem(code, 256), 0))

    def rows(zz, hh, cc, yy, size=16):
        return pl.ds(pl.multiple_of(yy * R + cc * 256 + zz * 32 + hh * 16, 16), size)

    def block(zz, hh, yy=y):
        return hx.at[rows(zz, hh, c, yy)]

    def pair(zz, cc=c, yy=y):
        return hx.at[rows(zz, 0, cc, yy, 32)]

    mine = block(z, h)
    hx[rows(z, h, c, y), 0:D] = packed
    hx[rows(z, h, c, y), D:HX] = extra.astype(F32).astype(BF16)
    pl.semaphore_wait(barrier, len(peers))

    up, down = at(zz=zs[1]), at(zz=zs[7])
    by_z, by_y, by_h = {}, {}, {}
    crossed = {}

    def cross(k, yy=y):
        crossed[k] = send(pair(zs[k], c, yy), pair(zs[k], c, yy), other_c)

    def spread_y(k):
        here = block(zs[k], h)
        by_y[k] = [send(here, here, device) for device in near_y]

    by_h[0] = send(mine, mine, other_h)
    for k in (4, 3, 5, 1, 7, 2, 6):
        by_z[(8 - k) % 8] = send(mine, mine, at(zz=zs[k]))
    spread_y(0)
    arrive(by_h[0], block(z, 1 - h))
    other = block(z, 1 - h)
    ups, downs = send(other, other, up), send(other, other, down)
    cross(0)
    for k in (4, 3, 5):
        here = block(zs[k], h)
        arrive(by_z[k], here)
        by_h[k] = send(here, here, other_h)
        spread_y(k)
    for k in (1, 7):
        arrive(by_z[k], block(zs[k], h))
    here = block(zs[7], 1 - h)
    arrive(ups, here)
    ups = send(here, here, up)
    cross(7)
    here = block(zs[1], 1 - h)
    arrive(downs, here)
    downs = send(here, here, down)
    cross(1)
    for ticket, hh in zip(by_y[0], (h, 1 - h)):
        arrive(ticket, block(z, hh, 1 - y))
    theirs0 = pair(z, c, 1 - y)
    by_zz = {7: send(theirs0, theirs0, up), 1: send(theirs0, theirs0, down)}
    first_other = send(theirs0, theirs0, other_c)
    for k in (2, 6):
        arrive(by_z[k], block(zs[k], h))
        spread_y(k)
    for k in (4, 3, 5):
        arrive(by_h[k], block(zs[k], 1 - h))
        cross(k)
    arrive(ups, block(zs[6], 1 - h))
    cross(6)
    arrive(downs, block(zs[2], 1 - h))
    cross(2)
    for k in (0, 7, 1, 4, 3, 5, 6, 2):
        arrive(crossed[k], pair(zs[k], 1 - c))
    weight_in.wait()

    own_lanes = pl.ds(pl.multiple_of(y * R, R), R)
    other_lanes = pl.ds(pl.multiple_of((1 - y) * R, R), R)

    def logits_of(k, lanes):
        at_k = slice(512 * k, 512 * (k + 1))
        lg[at_k, lanes] = nt(w[at_k, :], hx[lanes, 0:D])

    crossed = {0: first_other}

    def take_other(k):
        if k in (1, 7):
            arrive(by_zz[k], pair(zs[k], c, 1 - y))
        else:
            for ticket, hh in zip(by_y[k], (h, 1 - h)):
                arrive(ticket, block(zs[k], hh, 1 - y))
        cross(k, 1 - y)

    for k in range(2):
        logits_of(k, own_lanes)
        for kk in ((), ())[k]:
            take_other(kk)

    ones = lax.broadcasted_iota(jnp.int32, (8, 128), 0) == lax.broadcasted_iota(jnp.int32, (8, 128), 1)
    ones = ones.astype(F32).astype(BF16)

    def marks(lanes):
        halves = nt(ones, hx[lanes, D:HX])
        return (halves[0:1] * 256.0 + halves[1:2]).astype(jnp.int32) - me_v * VD

    marked = marks(own_lanes)
    top = jnp.max(lg[:, own_lanes], axis=0, keepdims=True)

    def sums_of(k, carry):
        total, named, share = carry
        at_k = pl.ds(pl.multiple_of(k * 64, 64), 64)
        part = lg[at_k, own_lanes]
        hit = lax.broadcasted_iota(jnp.int32, (64, R), 0) + k * 64 == marked
        named = named + jnp.sum(jnp.where(hit, part, 0.0), axis=0, keepdims=True)
        grown = jnp.exp(part - top)
        lg[at_k, own_lanes] = grown
        share = share + jnp.sum(jnp.where(hit, grown, 0.0), axis=0, keepdims=True)
        return total + jnp.sum(grown, axis=0, keepdims=True), named, share

    total, named, share = lax.fori_loop(
        0, VD // 64, sums_of, tuple(jnp.zeros((1, R), F32) for _ in range(3))
    )

    def fold(row):
        return jnp.concatenate([row[:, 128 * k : 128 * (k + 1)] for k in range(R // 128)], axis=0)

    def unfold(tile):
        return jnp.concatenate([tile[k : k + 1] for k in range(R // 128)], axis=1)

    def join(tops, totals, nameds):
        best = tops[0]
        for other_top in tops[1:]:
            best = jnp.maximum(best, other_top)
        total = sum(t * jnp.exp(m - best) for t, m in zip(totals, tops))
        return best, total, sum(nameds)

    def begin(triple, out_ref, in_ref, devices):
        out_ref[0:4], out_ref[4:8], out_ref[8:12] = triple
        out_ref[12:16] = jnp.zeros((4, 128), F32)
        return [send(out_ref, in_ref.at[k], device) for k, device in enumerate(devices)]

    def end(triple, in_ref, tickets):
        parts = [triple]
        for k, ticket in enumerate(tickets):
            arrive(ticket, in_ref.at[k])
            parts.append((in_ref[k, 0:4], in_ref[k, 4:8], in_ref[k, 8:12]))
        return join(*zip(*parts))

    def core_lanes(cc):
        return pl.ds(pl.multiple_of(y * R + cc * 256, 256), 256)

    triple = tuple(fold(row) for row in (top, total, named))
    tickets = begin(triple, st_mine, st_in, layer)
    for k in (1, 7, 2, 6, 4, 3, 5):
        take_other(k)

    code_row = hx[core_lanes(1 - c), D:HX].astype(F32)
    code_row = code_row[:, 0:1] * 256.0 + code_row[:, 1:2] - (me_v * VD).astype(F32)
    their_marks = marks(core_lanes(1 - c))

    def unnamed(k, _):
        at_k = pl.ds(pl.multiple_of(k * 128, 128), 128)
        code_at = lax.broadcasted_iota(jnp.int32, (128, 256), 0) + k * 128
        grown = jnp.where(code_at == their_marks, 0.0, lg[at_k, core_lanes(1 - c)])
        g[0:256, at_k] = grown.T.astype(BF16)
        code_at = lax.broadcasted_iota(jnp.int32, (256, 128), 1) + k * 128
        g[256:512, at_k] = (code_at.astype(F32) == code_row).astype(F32).astype(BF16)
        return 0

    lax.fori_loop(0, VD // 128, unnamed, 0)
    for k in range(8):
        arrive(crossed[k], pair(zs[k], 1 - c, 1 - y))
    logits_of(0, other_lanes)
    triple = end(triple, st_in, tickets)
    tickets = begin(triple, tot_mine, tot_in, column + across)
    logits_of(1, other_lanes)
    other_marked = marks(other_lanes)

    def theirs(k, _):
        at_k = pl.ds(pl.multiple_of(k * 512, 512), 512)
        ha[:, at_k] = nn(g[...], w[:, at_k])
        return 0

    lax.fori_loop(0, D // 512, theirs, 0)
    row_top, row_total, row_named = end(triple, tot_in, tickets[:7])
    log_total = row_top + jnp.log(row_total)

    factor = LOSS_SCALE * jnp.exp(top - unfold(log_total))
    both = jnp.concatenate([factor, factor * share - LOSS_SCALE, jnp.zeros((126, R), F32)], axis=0)
    fc[...] = jnp.where(c == 0, both[:, 256:512], both[:, 0:256]).T

    d_tickets = []
    for k in range(4):
        at_k = slice(512 * k, 512 * (k + 1))
        hd_out[k] = (fc[:, 0:1] * ha[0:256, at_k] + fc[:, 1:2] * ha[256:512, at_k]).astype(BF16)
        d_tickets.append(send(hd_out.at[k], hd_in.at[k], other_c))

    other_parts = []
    for k, ticket in enumerate(tickets[7:]):
        arrive(ticket, tot_in.at[7 + k])
        other_parts.append((tot_in[7 + k, 0:4], tot_in[7 + k, 4:8], tot_in[7 + k, 8:12]))
    other_top, other_sum, _ = join(*zip(*other_parts))
    other_total = unfold(other_top + jnp.log(other_sum))

    def grads_of(k, _):
        at_k = pl.ds(pl.multiple_of(k * 128, 128), 128)
        code_at = lax.broadcasted_iota(jnp.int32, (128, R), 0) + k * 128
        grad = lg[at_k, own_lanes] * factor - jnp.where(code_at == marked, LOSS_SCALE, 0.0)
        gt[at_k, own_lanes] = grad.astype(BF16)
        g[0:256, at_k] = jnp.where(c == 0, grad[:, 0:256], grad[:, 256:512]).T.astype(BF16)
        grad = jnp.exp(lg[at_k, other_lanes] - other_total)
        grad = LOSS_SCALE * (grad - jnp.where(code_at == other_marked, 1.0, 0.0))
        gt[at_k, other_lanes] = grad.astype(BF16)
        return 0

    def part(chunk, xx):
        start, size = chunk
        at_s = pl.ds(pl.multiple_of((y * 4 + xx) * CW, CW), CW)
        return nn(gt[start : start + size, :], hx[:, at_s])

    def halves_of(chunk):
        start, size = chunk
        return slice(start, start + size // 2), slice(start + size // 2, start + size)

    a_tickets, lr_tickets = [], []
    for chunk in CHUNKS:
        start, size = chunk
        lax.fori_loop(start // 128, (start + size) // 128, grads_of, 0)
        xs[0, start : start + size, :] = part(chunk, far_x).astype(BF16)
        a_tickets.append([
            send(xs.at[0, spot], xa_in.at[spot], at(xx=to))
            for spot, to in zip(halves_of(chunk), (right_x, left_x))
        ])

    for k, ticket in enumerate(d_tickets):
        at_k = slice(512 * k, 512 * (k + 1))
        ours = nn(g[0:256, :], w[:, at_k])
        arrive(ticket, hd_in.at[k])
        hacc[:, at_k] = ours + hd_in[k].astype(F32)

    def owner_rows(k, hh):
        return pl.ds(pl.multiple_of(zs[k] * 32 + hh * 16, 16), 16)

    p_tickets = []
    for i, k in enumerate((1, 7)):
        zp_out[i] = hacc[pl.ds(pl.multiple_of(zs[k] * 32, 32), 32), :].astype(BF16)
        p_tickets.append(send(zp_out.at[i], zp_in.at[i], at(zz=zs[k])))
    h_tickets = []
    for first, last in GROUPS:
        for slot in range(first, last):
            yo[slot] = hacc[owner_rows(FAR[slot], 1 - h), :].astype(BF16)
        h_tickets.append(send(yo.at[first:last], yi.at[first:last], other_h))

    z_tickets = {}

    def along_z(group):
        first, last = GROUPS[group]
        arrive(h_tickets[group], yi.at[first:last])
        for slot in range(first, last):
            k = FAR[slot]
            zo[slot] = (hacc[owner_rows(k, h), :] + yi[slot].astype(F32)).astype(BF16)
            z_tickets[slot] = send(zo.at[slot], zi.at[slot], at(zz=zs[k]))

    def near_sum(hh):
        at_h = pl.ds(pl.multiple_of(hh * 16, 16), 16)
        return hacc[owner_rows(0, hh), :] + zp_in[0, at_h, :].astype(F32) + zp_in[1, at_h, :].astype(F32)

    sides = ((right_x, xl_in), (left_x, xr_in))
    for k, chunk in enumerate(CHUNKS):
        spots, half = halves_of(chunk), chunk[1] // 2
        tickets = []
        for side, (to, into) in enumerate(sides):
            value = part(chunk, to)
            joined, plain = value[:half], value[half:]
            if side:
                joined, plain = plain, joined
            x_own[side, half * k : half * (k + 1), :] = joined
            spot = spots[1 - side]
            xs[1 + side, spot, :] = plain.astype(BF16)
            tickets.append((send(xs.at[1 + side, spot], into.at[spot], at(xx=to)), into.at[spot]))
        lr_tickets.append(tickets)
        if k == 1:
            along_z(0)

    for k, chunk in enumerate(CHUNKS):
        spots, half = halves_of(chunk), chunk[1] // 2
        for side, (to, into) in enumerate(sides):
            spot = spots[side]
            arrive(a_tickets[k][side], xa_in.at[spot])
            value = x_own[side, half * k : half * (k + 1), :] + xa_in[spot, :].astype(F32)
            xs[1 + side, spot, :] = value.astype(BF16)
            ticket = send(xs.at[1 + side, spot], into.at[spot], at(xx=to))
            lr_tickets[k].append((ticket, into.at[spot]))
        if k == 0:
            along_z(1)
        if k == 1:
            for i, ticket in enumerate(p_tickets):
                arrive(ticket, zp_in.at[i])
            yo[5] = near_sum(1 - h).astype(BF16)
            near_ticket = send(yo.at[5], yi.at[5], other_h)
        if k == 2:
            along_z(2)

    loss_mine[0:4] = log_total - row_named
    lanes8 = lax.broadcasted_iota(jnp.int32, (4, 128), 1)
    sends = jnp.zeros((4, 128), F32)
    for j in range(NS):
        sends = jnp.where(lanes8 == j, counts[0, 0, j].astype(F32), sends)
    loss_mine[4:8] = sends
    loss_tickets = [send(loss_mine, loss_in.at[k], device) for k, device in enumerate(others)]

    for _ in range(len(sent) - 20):
        sent.pop(0).wait_send()

    for chunk in CHUNKS:
        start, size = chunk
        code_own[start : start + size, :] = part(chunk, x)
    tiles = [loss_mine[...]]
    for k, ticket in enumerate(loss_tickets):
        arrive(ticket, loss_in.at[k])
        tiles.append(loss_in[k])
    lane1 = lax.broadcasted_iota(jnp.int32, (1, 128), 1)
    own_row = lax.broadcasted_iota(jnp.int32, (4, 128), 0) == (c * 2 + z // 4)
    rank = lane1 - (lax.rem(z, 4) * 32 + h * 16)
    in_block = (rank >= 0) & (rank < RD)
    slots = lax.broadcasted_iota(jnp.int32, (RD, 128), 0)
    got, before, losses = [], [], []
    for tile in tiles:
        row = tile[4:5]
        got.append(jnp.sum(jnp.where(lane1 == me_s, row, 0.0), axis=1, keepdims=True).astype(jnp.int32))
        before.append(jnp.sum(jnp.where(lane1 < me_s, row, 0.0), axis=1, keepdims=True).astype(jnp.int32))
        losses.append(jnp.sum(jnp.where(own_row, tile[0:4], 0.0), axis=0, keepdims=True))
    listed = jnp.zeros((RD, 128), F32)
    for k in range(NS):
        source = lax.rem(me_s + NS - k, NS)
        first = jnp.zeros((1, 1), jnp.int32)
        for j in range(NS):
            earlier = lax.rem(me_s + NS - j, NS) < source
            first = first + jnp.where(earlier, got[j], 0)
        offset = rank - before[k]
        live = in_block & (offset >= 0) & (offset < got[k])
        slot = jnp.where(live, first + offset, -1)
        listed = listed + jnp.where(slots == slot, losses[k], 0.0)
    turned = jnp.concatenate([listed, jnp.zeros((128 - RD, 128), F32)], axis=0).T
    loss_out[0] = jnp.sum(turned, axis=0, keepdims=True)[:, 0:RD]

    for k, chunk in enumerate(CHUNKS):
        start, size = chunk
        spot = slice(start, start + size)
        value = code_own[spot, :]
        for ticket, where in lr_tickets[k]:
            arrive(ticket, where)
        value = value + xl_in[spot, :].astype(F32) + xr_in[spot, :].astype(F32)
        code_out[spot, :] = value.astype(BF16)

    arrive(near_ticket, yi.at[5])
    own = near_sum(h) + yi[5].astype(F32)
    for slot in range(5):
        arrive(z_tickets[slot], zi.at[slot])
        own = own + zi[slot].astype(F32)
    spread = position((2 * RD, RD), 1) == lax.broadcasted_iota(jnp.int32, (2 * RD, RD), 0)
    hid_out[...] = nn(spread.astype(F32).astype(BF16), own.astype(BF16)).astype(BF16)

    for copy in sent:
        copy.wait_send()


def per_device(hidden, head_weight, targets, span_counts, send_counts):
    vmem, smem = pl.BlockSpec(memory_space=pltpu.VMEM), pl.BlockSpec(memory_space=pltpu.SMEM)
    copies = 192
    code_grad, hidden_grad, listed = pl.pallas_call(
        body,
        out_shape=(
            pltpu.VMEM((VD, CW), BF16),
            pltpu.VMEM((2 * RD, D), BF16),
            pltpu.VMEM((1, 1, RD), F32),
        ),
        in_specs=[smem, smem, smem, pl.BlockSpec(memory_space=pl.ANY), pl.BlockSpec(memory_space=pl.ANY)],
        out_specs=(vmem, vmem, vmem),
        scratch_shapes=[
            pltpu.VMEM((VD, D), BF16),
            pltpu.VMEM((2 * R, HX), BF16),
            pltpu.VMEM((VD, 2 * R), F32),
            pltpu.VMEM((VD, 2 * R), BF16),
            pltpu.VMEM((512, VD), BF16),
            pltpu.VMEM((256, 128), F32),
            pltpu.VMEM((16, 128), F32),
            pltpu.VMEM((3, 16, 128), F32),
            pltpu.VMEM((16, 128), F32),
            pltpu.VMEM((15, 16, 128), F32),
            pltpu.VMEM((8, 128), F32),
            pltpu.VMEM((7, 8, 128), F32),
            pltpu.VMEM((3, VD, CW), BF16),
            pltpu.VMEM((VD, CW), BF16),
            pltpu.VMEM((VD, CW), BF16),
            pltpu.VMEM((VD, CW), BF16),
            pltpu.VMEM((2, VD // 2, CW), F32),
            pltpu.VMEM((VD, CW), F32),
            pltpu.VMEM((512, D), F32),
            pltpu.VMEM((4, 256, 512), BF16),
            pltpu.VMEM((4, 256, 512), BF16),
            pltpu.VMEM((256, D), F32),
            pltpu.VMEM((6, RD, D), BF16),
            pltpu.VMEM((6, RD, D), BF16),
            pltpu.VMEM((5, RD, D), BF16),
            pltpu.VMEM((5, RD, D), BF16),
            pltpu.VMEM((2, 2 * RD, D), BF16),
            pltpu.VMEM((2, 2 * RD, D), BF16),
            pltpu.VMEM((1, 1, 2, RD, D), BF16),
            pltpu.SemaphoreType.DMA((copies,)),
            pltpu.SemaphoreType.DMA((copies,)),
            pltpu.SemaphoreType.DMA((2,)),
        ],
        compiler_params=pltpu.CompilerParams(
            collective_id=0, has_side_effects=True, vmem_limit_bytes=56 * 1024 * 1024
        ),
        name="head",
    )(span_counts, send_counts, targets, hidden, head_weight)
    code_grad, hidden_grad, losses = pl.pallas_call(
        hand_over,
        out_shape=(
            jax.ShapeDtypeStruct((VD, CW), BF16),
            jax.ShapeDtypeStruct((2 * RD, D), BF16),
            jax.ShapeDtypeStruct((1, 1, RD), F32),
        ),
        in_specs=[vmem] * 3,
        out_specs=(vmem,) * 3,
        name="hand_over",
    )(*(pltpu.with_memory_space_constraint(a, pltpu.VMEM) for a in (code_grad, hidden_grad, listed)))
    return losses, hidden_grad.reshape(hidden.shape), code_grad


def hand_over(code_in, hid_in, loss_in, code_out, hid_out, loss_out):
    code_out[...] = code_in[...]
    hid_out[...] = hid_in[...]
    loss_out[...] = loss_in[...]


def solution(mesh):
    in_specs = (
        P("seq", "vocab", None, None, None),
        P("vocab", None),
        P("seq", "vocab", None, None),
        P("seq", "vocab", None),
        P("seq", "vocab", None),
    )
    out_specs = (P("seq", "vocab", None), P("seq", "vocab", None, None, None), P("vocab", "seq"))
    return jax.shard_map(
        per_device, mesh=mesh, in_specs=in_specs, out_specs=out_specs, check_vma=False
    )
```

```python
import itertools

import jax
import jax.numpy as jnp
from jax import lax
from jax.experimental import pallas as pl
from jax.experimental.pallas import tpu as pltpu
from jax.sharding import PartitionSpec as P

LOSS_SCALE = 4.0
D = 2048
VD = 1024
RD = 16
NV = 32
R = RD * NV
NS = 8
CW = D // NS
HX = D + 128
CHUNKS = [(256 * k, 256) for k in range(4)]
FAR = (4, 3, 5, 2, 6)
GROUPS = ((0, 1), (1, 3), (3, 5))
F32, BF16 = jnp.float32, jnp.bfloat16
MESH = pl.DeviceIdType.MESH


def nt(a, b):
    return lax.dot_general(a, b, (((1,), (1,)), ((), ())), preferred_element_type=F32)


def nn(a, b):
    return jnp.dot(a, b, preferred_element_type=F32)


def body(
    spans, counts, targets, hidden_at, weight,
    code_out, hid_out, loss_out,
    w, hx, lg, gt, g,
    fc, st_mine, st_in, tot_mine, tot_in, loss_mine, loss_in,
    xs, xa_in, xl_in, xr_in,
    x_own, code_own, ha, hd_out, hd_in, hacc, yo, yi, zo, zi, zp_out, zp_in,
    hidden, ssem, rsem, wsem,
):
    me_s, me_v = lax.axis_index("seq"), lax.axis_index("vocab")
    x, y = lax.rem(me_s, 4), me_s // 4
    z, h, c = me_v // 4, lax.rem(me_v // 2, 2), lax.rem(me_v, 2)
    ids = itertools.count()
    sent = []

    def at(xx=None, yy=None, zz=None, hh=None, cc=None):
        xx, yy, zz, hh, cc = (
            mine if other is None else other
            for other, mine in ((xx, x), (yy, y), (zz, z), (hh, h), (cc, c))
        )
        return {"seq": yy * 4 + xx, "vocab": zz * 4 + hh * 2 + cc}

    def send(src, dst, device):
        i = next(ids)
        copy = pltpu.make_async_remote_copy(
            src_ref=src, dst_ref=dst, send_sem=ssem.at[i], recv_sem=rsem.at[i],
            device_id=device, device_id_type=MESH,
        )
        copy.start()
        sent.append(copy)
        return i, device

    def arrive(ticket, where):
        i, device = ticket
        pltpu.make_async_remote_copy(
            src_ref=where, dst_ref=where, send_sem=ssem.at[i], recv_sem=rsem.at[i],
            device_id=device, device_id_type=MESH,
        ).wait_recv()

    right_x, left_x, far_x = (lax.rem(x + k, 4) for k in (1, 3, 2))
    zs = [lax.rem(z + k, 8) for k in range(8)]
    other_c, other_h = at(cc=1 - c), at(hh=1 - h)
    near_y = [at(yy=1 - y), at(yy=1 - y, hh=1 - h)]
    layer = [other_c, other_h, at(hh=1 - h, cc=1 - c)]
    column = [at(zz=zs[k]) for k in (4, 3, 5, 2, 6, 1, 7)]
    others = [
        {"seq": lax.rem(me_s + k, NS), "vocab": me_v} for k in range(1, NS)
    ]
    across = [at(yy=1 - y, zz=zs[k]) for k in (4, 3, 5, 2, 6, 1, 7, 0)]
    peers = layer + column + others + near_y[1:] + across[:7]

    hidden_in = pltpu.make_async_copy(hidden_at, hidden, wsem.at[0])
    hidden_in.start()
    barrier = pltpu.get_barrier_semaphore()
    for device in peers:
        pl.semaphore_signal(barrier, inc=1, device_id=device, device_id_type=MESH)
    weight_in = pltpu.make_async_copy(weight, w, wsem.at[1])
    weight_in.start()

    s0 = spans[0, 0, 0]

    def position(shape, axis):
        rank = lax.broadcasted_iota(jnp.int32, shape, axis)
        return jnp.where(rank < s0, RD - s0 + rank, RD + rank)

    pick = position((RD, 2 * RD), 0) == lax.broadcasted_iota(jnp.int32, (RD, 2 * RD), 1)
    hidden_in.wait()
    packed = nn(pick.astype(F32).astype(BF16), hidden[0, 0].reshape(2 * RD, D)).astype(BF16)
    place = position((RD, 128), 0)
    code = jnp.zeros((RD, 128), jnp.int32)
    for q in range(2):
        for p in range(RD):
            code = jnp.where(place == q * RD + p, targets[0, 0, q, p], code)
    lane = lax.broadcasted_iota(jnp.int32, (RD, 128), 1)
    extra = jnp.where(lane == 0, code // 256, jnp.where(lane == 1, lax.rem(code, 256), 0))

    def rows(zz, hh, cc, yy, size=16):
        return pl.ds(pl.multiple_of(yy * R + cc * 256 + zz * 32 + hh * 16, 16), size)

    def block(zz, hh, yy=y):
        return hx.at[rows(zz, hh, c, yy)]

    def pair(zz, cc=c, yy=y):
        return hx.at[rows(zz, 0, cc, yy, 32)]

    mine = block(z, h)
    hx[rows(z, h, c, y), 0:D] = packed
    hx[rows(z, h, c, y), D:HX] = extra.astype(F32).astype(BF16)
    pl.semaphore_wait(barrier, len(peers))

    up, down = at(zz=zs[1]), at(zz=zs[7])
    by_z, by_y, by_h = {}, {}, {}
    crossed = {}

    def cross(k, yy=y):
        crossed[k] = send(pair(zs[k], c, yy), pair(zs[k], c, yy), other_c)

    def spread_y(k):
        here = block(zs[k], h)
        by_y[k] = [send(here, here, device) for device in near_y]

    by_h[0] = send(mine, mine, other_h)
    for k in (4, 3, 5, 1, 7, 2, 6):
        by_z[(8 - k) % 8] = send(mine, mine, at(zz=zs[k]))
    spread_y(0)
    arrive(by_h[0], block(z, 1 - h))
    other = block(z, 1 - h)
    ups, downs = send(other, other, up), send(other, other, down)
    cross(0)
    for k in (4, 3, 5):
        here = block(zs[k], h)
        arrive(by_z[k], here)
        by_h[k] = send(here, here, other_h)
    for k in (4, 3, 5):
        spread_y(k)
    for k in (1, 7):
        arrive(by_z[k], block(zs[k], h))
    here = block(zs[7], 1 - h)
    arrive(ups, here)
    ups = send(here, here, up)
    cross(7)
    here = block(zs[1], 1 - h)
    arrive(downs, here)
    downs = send(here, here, down)
    cross(1)
    for ticket, hh in zip(by_y[0], (h, 1 - h)):
        arrive(ticket, block(z, hh, 1 - y))
    theirs0 = pair(z, c, 1 - y)
    by_zz = {7: send(theirs0, theirs0, up), 1: send(theirs0, theirs0, down)}
    first_other = send(theirs0, theirs0, other_c)
    for k in (2, 6):
        arrive(by_z[k], block(zs[k], h))
        spread_y(k)
    for k in (4, 3, 5):
        arrive(by_h[k], block(zs[k], 1 - h))
        cross(k)
    arrive(ups, block(zs[6], 1 - h))
    cross(6)
    arrive(downs, block(zs[2], 1 - h))
    cross(2)
    for k in (0, 7, 1, 4, 3, 5, 6, 2):
        arrive(crossed[k], pair(zs[k], 1 - c))
    weight_in.wait()

    own_lanes = pl.ds(pl.multiple_of(y * R, R), R)
    other_lanes = pl.ds(pl.multiple_of((1 - y) * R, R), R)

    def logits_of(k, lanes):
        at_k = slice(512 * k, 512 * (k + 1))
        lg[at_k, lanes] = nt(w[at_k, :], hx[lanes, 0:D])

    crossed = {0: first_other}

    def take_other(k):
        if k in (1, 7):
            arrive(by_zz[k], pair(zs[k], c, 1 - y))
        else:
            for ticket, hh in zip(by_y[k], (h, 1 - h)):
                arrive(ticket, block(zs[k], hh, 1 - y))
        cross(k, 1 - y)

    for k in range(2):
        logits_of(k, own_lanes)

    ones = lax.broadcasted_iota(jnp.int32, (8, 128), 0) == lax.broadcasted_iota(jnp.int32, (8, 128), 1)
    ones = ones.astype(F32).astype(BF16)

    def marks(lanes):
        halves = nt(ones, hx[lanes, D:HX])
        return (halves[0:1] * 256.0 + halves[1:2]).astype(jnp.int32) - me_v * VD

    marked = marks(own_lanes)
    top = jnp.max(lg[:, own_lanes], axis=0, keepdims=True)

    def sums_of(k, carry):
        total, named, share = carry
        at_k = pl.ds(pl.multiple_of(k * 64, 64), 64)
        part = lg[at_k, own_lanes]
        hit = lax.broadcasted_iota(jnp.int32, (64, R), 0) + k * 64 == marked
        named = named + jnp.sum(jnp.where(hit, part, 0.0), axis=0, keepdims=True)
        grown = jnp.exp(part - top)
        lg[at_k, own_lanes] = grown
        share = share + jnp.sum(jnp.where(hit, grown, 0.0), axis=0, keepdims=True)
        return total + jnp.sum(grown, axis=0, keepdims=True), named, share

    total, named, share = lax.fori_loop(
        0, VD // 64, sums_of, tuple(jnp.zeros((1, R), F32) for _ in range(3))
    )

    def fold(row):
        return jnp.concatenate([row[:, 128 * k : 128 * (k + 1)] for k in range(R // 128)], axis=0)

    def unfold(tile):
        return jnp.concatenate([tile[k : k + 1] for k in range(R // 128)], axis=1)

    def join(tops, totals, nameds):
        best = tops[0]
        for other_top in tops[1:]:
            best = jnp.maximum(best, other_top)
        total = sum(t * jnp.exp(m - best) for t, m in zip(totals, tops))
        return best, total, sum(nameds)

    def begin(triple, out_ref, in_ref, devices):
        out_ref[0:4], out_ref[4:8], out_ref[8:12] = triple
        out_ref[12:16] = jnp.zeros((4, 128), F32)
        return [send(out_ref, in_ref.at[k], device) for k, device in enumerate(devices)]

    def end(triple, in_ref, tickets):
        parts = [triple]
        for k, ticket in enumerate(tickets):
            arrive(ticket, in_ref.at[k])
            parts.append((in_ref[k, 0:4], in_ref[k, 4:8], in_ref[k, 8:12]))
        return join(*zip(*parts))

    def core_lanes(cc):
        return pl.ds(pl.multiple_of(y * R + cc * 256, 256), 256)

    triple = tuple(fold(row) for row in (top, total, named))
    tickets = begin(triple, st_mine, st_in, layer)
    for k in (1, 7, 2, 6, 4, 3, 5):
        take_other(k)

    code_row = hx[core_lanes(1 - c), D:HX].astype(F32)
    code_row = code_row[:, 0:1] * 256.0 + code_row[:, 1:2] - (me_v * VD).astype(F32)
    their_marks = marks(core_lanes(1 - c))

    def unnamed(k, _):
        at_k = pl.ds(pl.multiple_of(k * 128, 128), 128)
        code_at = lax.broadcasted_iota(jnp.int32, (128, 256), 0) + k * 128
        grown = jnp.where(code_at == their_marks, 0.0, lg[at_k, core_lanes(1 - c)])
        g[0:256, at_k] = grown.T.astype(BF16)
        code_at = lax.broadcasted_iota(jnp.int32, (256, 128), 1) + k * 128
        g[256:512, at_k] = (code_at.astype(F32) == code_row).astype(F32).astype(BF16)
        return 0

    lax.fori_loop(0, VD // 128, unnamed, 0)
    for k in range(8):
        arrive(crossed[k], pair(zs[k], 1 - c, 1 - y))
    logits_of(0, other_lanes)
    triple = end(triple, st_in, tickets)
    tickets = begin(triple, tot_mine, tot_in, column + across)
    logits_of(1, other_lanes)
    other_marked = marks(other_lanes)

    def theirs(k, _):
        at_k = pl.ds(pl.multiple_of(k * 512, 512), 512)
        ha[:, at_k] = nn(g[...], w[:, at_k])
        return 0

    lax.fori_loop(0, D // 512, theirs, 0)
    row_top, row_total, row_named = end(triple, tot_in, tickets[:7])
    log_total = row_top + jnp.log(row_total)

    factor = LOSS_SCALE * jnp.exp(top - unfold(log_total))
    both = jnp.concatenate([factor, factor * share - LOSS_SCALE, jnp.zeros((126, R), F32)], axis=0)
    fc[...] = jnp.where(c == 0, both[:, 256:512], both[:, 0:256]).T

    d_tickets = []
    for k in range(4):
        at_k = slice(512 * k, 512 * (k + 1))
        hd_out[k] = (fc[:, 0:1] * ha[0:256, at_k] + fc[:, 1:2] * ha[256:512, at_k]).astype(BF16)
        d_tickets.append(send(hd_out.at[k], hd_in.at[k], other_c))

    other_parts = []
    for k, ticket in enumerate(tickets[7:]):
        arrive(ticket, tot_in.at[7 + k])
        other_parts.append((tot_in[7 + k, 0:4], tot_in[7 + k, 4:8], tot_in[7 + k, 8:12]))
    other_top, other_sum, _ = join(*zip(*other_parts))
    other_total = unfold(other_top + jnp.log(other_sum))

    def grads_of(k, _):
        at_k = pl.ds(pl.multiple_of(k * 128, 128), 128)
        code_at = lax.broadcasted_iota(jnp.int32, (128, R), 0) + k * 128
        grad = lg[at_k, own_lanes] * factor - jnp.where(code_at == marked, LOSS_SCALE, 0.0)
        gt[at_k, own_lanes] = grad.astype(BF16)
        g[0:256, at_k] = jnp.where(c == 0, grad[:, 0:256], grad[:, 256:512]).T.astype(BF16)
        grad = jnp.exp(lg[at_k, other_lanes] - other_total)
        grad = LOSS_SCALE * (grad - jnp.where(code_at == other_marked, 1.0, 0.0))
        gt[at_k, other_lanes] = grad.astype(BF16)
        return 0

    def part(chunk, xx):
        start, size = chunk
        at_s = pl.ds(pl.multiple_of((y * 4 + xx) * CW, CW), CW)
        return nn(gt[start : start + size, :], hx[:, at_s])

    def halves_of(chunk):
        start, size = chunk
        return slice(start, start + size // 2), slice(start + size // 2, start + size)

    a_tickets, lr_tickets = [], []
    for chunk in CHUNKS:
        start, size = chunk
        lax.fori_loop(start // 128, (start + size) // 128, grads_of, 0)
        xs[0, start : start + size, :] = part(chunk, far_x).astype(BF16)
        a_tickets.append([
            send(xs.at[0, spot], xa_in.at[spot], at(xx=to))
            for spot, to in zip(halves_of(chunk), (right_x, left_x))
        ])

    for k, ticket in enumerate(d_tickets):
        at_k = slice(512 * k, 512 * (k + 1))
        ours = nn(g[0:256, :], w[:, at_k])
        arrive(ticket, hd_in.at[k])
        hacc[:, at_k] = ours + hd_in[k].astype(F32)

    def owner_rows(k, hh):
        return pl.ds(pl.multiple_of(zs[k] * 32 + hh * 16, 16), 16)

    p_tickets = []
    for i, k in enumerate((1, 7)):
        zp_out[i] = hacc[pl.ds(pl.multiple_of(zs[k] * 32, 32), 32), :].astype(BF16)
        p_tickets.append(send(zp_out.at[i], zp_in.at[i], at(zz=zs[k])))
    h_tickets = []
    for first, last in GROUPS:
        for slot in range(first, last):
            yo[slot] = hacc[owner_rows(FAR[slot], 1 - h), :].astype(BF16)
        h_tickets.append(send(yo.at[first:last], yi.at[first:last], other_h))

    z_tickets = {}

    def along_z(group):
        first, last = GROUPS[group]
        arrive(h_tickets[group], yi.at[first:last])
        for slot in range(first, last):
            k = FAR[slot]
            zo[slot] = (hacc[owner_rows(k, h), :] + yi[slot].astype(F32)).astype(BF16)
            z_tickets[slot] = send(zo.at[slot], zi.at[slot], at(zz=zs[k]))

    def near_sum(hh):
        at_h = pl.ds(pl.multiple_of(hh * 16, 16), 16)
        return hacc[owner_rows(0, hh), :] + zp_in[0, at_h, :].astype(F32) + zp_in[1, at_h, :].astype(F32)

    sides = ((right_x, xl_in), (left_x, xr_in))
    for k, chunk in enumerate(CHUNKS):
        spots, half = halves_of(chunk), chunk[1] // 2
        tickets = []
        for side, (to, into) in enumerate(sides):
            value = part(chunk, to)
            joined, plain = value[:half], value[half:]
            if side:
                joined, plain = plain, joined
            x_own[side, half * k : half * (k + 1), :] = joined
            spot = spots[1 - side]
            xs[1 + side, spot, :] = plain.astype(BF16)
            tickets.append((send(xs.at[1 + side, spot], into.at[spot], at(xx=to)), into.at[spot]))
        lr_tickets.append(tickets)
        if k == 1:
            along_z(0)

    for k, chunk in enumerate(CHUNKS):
        spots, half = halves_of(chunk), chunk[1] // 2
        for side, (to, into) in enumerate(sides):
            spot = spots[side]
            arrive(a_tickets[k][side], xa_in.at[spot])
            value = x_own[side, half * k : half * (k + 1), :] + xa_in[spot, :].astype(F32)
            xs[1 + side, spot, :] = value.astype(BF16)
            ticket = send(xs.at[1 + side, spot], into.at[spot], at(xx=to))
            lr_tickets[k].append((ticket, into.at[spot]))
        if k == 0:
            along_z(1)
        if k == 1:
            for i, ticket in enumerate(p_tickets):
                arrive(ticket, zp_in.at[i])
            yo[5] = near_sum(1 - h).astype(BF16)
            near_ticket = send(yo.at[5], yi.at[5], other_h)
        if k == 2:
            along_z(2)

    loss_mine[0:4] = log_total - row_named
    lanes8 = lax.broadcasted_iota(jnp.int32, (4, 128), 1)
    sends = jnp.zeros((4, 128), F32)
    for j in range(NS):
        sends = jnp.where(lanes8 == j, counts[0, 0, j].astype(F32), sends)
    loss_mine[4:8] = sends
    loss_tickets = [send(loss_mine, loss_in.at[k], device) for k, device in enumerate(others)]

    for _ in range(len(sent) - 20):
        sent.pop(0).wait_send()

    for chunk in CHUNKS:
        start, size = chunk
        code_own[start : start + size, :] = part(chunk, x)
    tiles = [loss_mine[...]]
    for k, ticket in enumerate(loss_tickets):
        arrive(ticket, loss_in.at[k])
        tiles.append(loss_in[k])
    lane1 = lax.broadcasted_iota(jnp.int32, (1, 128), 1)
    own_row = lax.broadcasted_iota(jnp.int32, (4, 128), 0) == (c * 2 + z // 4)
    rank = lane1 - (lax.rem(z, 4) * 32 + h * 16)
    in_block = (rank >= 0) & (rank < RD)
    slots = lax.broadcasted_iota(jnp.int32, (RD, 128), 0)
    got, before, losses = [], [], []
    for tile in tiles:
        row = tile[4:5]
        got.append(jnp.sum(jnp.where(lane1 == me_s, row, 0.0), axis=1, keepdims=True).astype(jnp.int32))
        before.append(jnp.sum(jnp.where(lane1 < me_s, row, 0.0), axis=1, keepdims=True).astype(jnp.int32))
        losses.append(jnp.sum(jnp.where(own_row, tile[0:4], 0.0), axis=0, keepdims=True))
    listed = jnp.zeros((RD, 128), F32)
    for k in range(NS):
        source = lax.rem(me_s + NS - k, NS)
        first = jnp.zeros((1, 1), jnp.int32)
        for j in range(NS):
            earlier = lax.rem(me_s + NS - j, NS) < source
            first = first + jnp.where(earlier, got[j], 0)
        offset = rank - before[k]
        live = in_block & (offset >= 0) & (offset < got[k])
        slot = jnp.where(live, first + offset, -1)
        listed = listed + jnp.where(slots == slot, losses[k], 0.0)
    turned = jnp.concatenate([listed, jnp.zeros((128 - RD, 128), F32)], axis=0).T
    loss_out[0] = jnp.sum(turned, axis=0, keepdims=True)[:, 0:RD]

    for k, chunk in enumerate(CHUNKS):
        start, size = chunk
        spot = slice(start, start + size)
        value = code_own[spot, :]
        for ticket, where in lr_tickets[k]:
            arrive(ticket, where)
        value = value + xl_in[spot, :].astype(F32) + xr_in[spot, :].astype(F32)
        code_out[spot, :] = value.astype(BF16)

    arrive(near_ticket, yi.at[5])
    own = near_sum(h) + yi[5].astype(F32)
    for slot in range(5):
        arrive(z_tickets[slot], zi.at[slot])
        own = own + zi[slot].astype(F32)
    spread = position((2 * RD, RD), 1) == lax.broadcasted_iota(jnp.int32, (2 * RD, RD), 0)
    hid_out[...] = nn(spread.astype(F32).astype(BF16), own.astype(BF16)).astype(BF16)

    for copy in sent:
        copy.wait_send()


def per_device(hidden, head_weight, targets, span_counts, send_counts):
    vmem, smem = pl.BlockSpec(memory_space=pltpu.VMEM), pl.BlockSpec(memory_space=pltpu.SMEM)
    copies = 192
    code_grad, hidden_grad, listed = pl.pallas_call(
        body,
        out_shape=(
            pltpu.VMEM((VD, CW), BF16),
            pltpu.VMEM((2 * RD, D), BF16),
            pltpu.VMEM((1, 1, RD), F32),
        ),
        in_specs=[smem, smem, smem, pl.BlockSpec(memory_space=pl.ANY), pl.BlockSpec(memory_space=pl.ANY)],
        out_specs=(vmem, vmem, vmem),
        scratch_shapes=[
            pltpu.VMEM((VD, D), BF16),
            pltpu.VMEM((2 * R, HX), BF16),
            pltpu.VMEM((VD, 2 * R), F32),
            pltpu.VMEM((VD, 2 * R), BF16),
            pltpu.VMEM((512, VD), BF16),
            pltpu.VMEM((256, 128), F32),
            pltpu.VMEM((16, 128), F32),
            pltpu.VMEM((3, 16, 128), F32),
            pltpu.VMEM((16, 128), F32),
            pltpu.VMEM((15, 16, 128), F32),
            pltpu.VMEM((8, 128), F32),
            pltpu.VMEM((7, 8, 128), F32),
            pltpu.VMEM((3, VD, CW), BF16),
            pltpu.VMEM((VD, CW), BF16),
            pltpu.VMEM((VD, CW), BF16),
            pltpu.VMEM((VD, CW), BF16),
            pltpu.VMEM((2, VD // 2, CW), F32),
            pltpu.VMEM((VD, CW), F32),
            pltpu.VMEM((512, D), F32),
            pltpu.VMEM((4, 256, 512), BF16),
            pltpu.VMEM((4, 256, 512), BF16),
            pltpu.VMEM((256, D), F32),
            pltpu.VMEM((6, RD, D), BF16),
            pltpu.VMEM((6, RD, D), BF16),
            pltpu.VMEM((5, RD, D), BF16),
            pltpu.VMEM((5, RD, D), BF16),
            pltpu.VMEM((2, 2 * RD, D), BF16),
            pltpu.VMEM((2, 2 * RD, D), BF16),
            pltpu.VMEM((1, 1, 2, RD, D), BF16),
            pltpu.SemaphoreType.DMA((copies,)),
            pltpu.SemaphoreType.DMA((copies,)),
            pltpu.SemaphoreType.DMA((2,)),
        ],
        compiler_params=pltpu.CompilerParams(
            collective_id=0, has_side_effects=True, vmem_limit_bytes=56 * 1024 * 1024
        ),
        name="head",
    )(span_counts, send_counts, targets, hidden, head_weight)
    code_grad, hidden_grad, losses = pl.pallas_call(
        hand_over,
        out_shape=(
            jax.ShapeDtypeStruct((VD, CW), BF16),
            jax.ShapeDtypeStruct((2 * RD, D), BF16),
            jax.ShapeDtypeStruct((1, 1, RD), F32),
        ),
        in_specs=[vmem] * 3,
        out_specs=(vmem,) * 3,
        name="hand_over",
    )(*(pltpu.with_memory_space_constraint(a, pltpu.VMEM) for a in (code_grad, hidden_grad, listed)))
    return losses, hidden_grad.reshape(hidden.shape), code_grad


def hand_over(code_in, hid_in, loss_in, code_out, hid_out, loss_out):
    code_out[...] = code_in[...]
    hid_out[...] = hid_in[...]
    loss_out[...] = loss_in[...]


def solution(mesh):
    in_specs = (
        P("seq", "vocab", None, None, None),
        P("vocab", None),
        P("seq", "vocab", None, None),
        P("seq", "vocab", None),
        P("seq", "vocab", None),
    )
    out_specs = (P("seq", "vocab", None), P("seq", "vocab", None, None, None), P("vocab", "seq"))
    return jax.shard_map(
        per_device, mesh=mesh, in_specs=in_specs, out_specs=out_specs, check_vma=False
    )
```
